256 devices in a mesh: dp: 32 (over y_lo, z, core), head: 8 (over y_hi, x).
Axes of the slice: x: 4, y: 4 (y_hi: 2, y_lo: 2; y = y_hi * 2 + y_lo), z: 8, core: 2. Of those that a mesh axis runs over, the one named last changes fastest.
Arguments:
- queries: bfloat16 [32, 2048, 2048], P('dp', 'head'), may hold values from -6 to 6
- key_states: bfloat16 [32, 2048, 2048], P('dp', 'head'), may hold values from -6 to 6
- value_states: bfloat16 [32, 2048, 2048], P('dp', 'head'), may hold values from -6 to 6
- queries_dot: bfloat16 [32, 2048, 2048], P('dp', 'head'), may hold values from -6 to 6
- keys_dot: bfloat16 [32, 2048, 2048], P('dp', 'head'), may hold values from -6 to 6
- values_dot: bfloat16 [32, 2048, 2048], P('dp', 'head'), may hold values from -6 to 6
- velocity: bfloat16 [32, 2048, 3072], P('dp', 'head'), may hold values from -3 to 3
- time_gap: float32 [32], P('dp'), may hold values from 0.3 to 1
- merge_slot: int32 [32, 2048], P('dp', 'head'), may hold values from 0 to 127, as said below
- out_weight: bfloat16 [3072, 2048], P(('dp', 'head')), may hold values from -0.125 to 0.125
Outputs:
- grad_attn: bfloat16 [32, 1024, 2048], P('dp', None, 'head')
- grad_weight: float32 [3072, 2048], P('dp', 'head')
The draws below stay inside these ranges and needn't reach their ends.
Inputs may be any that keep to these rules, and one draw needn't show every extreme that they name: `merge_slot`: within each aligned block of 256 source tokens of a clip the values name merged tokens of that block; the source at position 2 m of a block names m, so every merged token has at least one source.
All inputs are finite; a program needn't handle non-finite values.
Results may differ from the reference program's by a relative error of at most 0.0075.
Values may be sent and summed in bfloat16 or wider, within the bound.
A program may use at most 128 MiB of HBM per device.

```python
import math
import jax
import jax.numpy as jnp
from jax import lax

D = 3072
HEADS = 16
HD = 128
SRC_DEV = 256
MRG_DEV = 128
F = 2048
CLIPS = 32
SRC = 2048
MERGED = 1024
N_HEAD = 8


def draw_queries(key, part):
    key = jax.random.fold_in(key, 1)
    first = jax.random.fold_in(key, 0)
    values = jnp.clip(jax.random.normal(first, (CLIPS, SRC, F), jnp.float32), -6.0, 6.0)
    return values.astype(jnp.bfloat16)


def draw_key_states(key, part):
    key = jax.random.fold_in(key, 2)
    first = jax.random.fold_in(key, 0)
    values = jnp.clip(jax.random.normal(first, (CLIPS, SRC, F), jnp.float32), -6.0, 6.0)
    return values.astype(jnp.bfloat16)


def draw_merge_slot(key, part):
    key = jax.random.fold_in(key, 3)
    picks = jax.random.randint(key, (CLIPS, SRC), 0, MRG_DEV, dtype=jnp.int32)
    position = jnp.arange(SRC, dtype=jnp.int32) % SRC_DEV
    kept = jnp.broadcast_to(position // 2, (CLIPS, SRC))
    return jnp.where(position % 2 == 0, kept, picks).astype(jnp.int32)


def block_levels(own_key, extent, shards, least, high):
    gain = 1.0
    for axis_at, blocks in shards:
        steps = jax.random.uniform(jax.random.fold_in(jax.random.fold_in(own_key, 6), axis_at), (blocks,), jnp.float32, least / len(shards), high / len(shards))
        gain = gain * jnp.repeat(jnp.exp(steps), extent[axis_at] // blocks).reshape((-1,) + (1,) * (len(extent) - 1 - axis_at))
    return gain


def gaussian(stream_key, shape, scale, most, shards=(), kind=jnp.bfloat16):
    array = scale * jax.random.normal(stream_key, shape, jnp.float32)
    if shards:
        array = array * block_levels(stream_key, shape, shards, -0.22, 0.18)
    return jnp.clip(array, -most, most).astype(kind)


def setup_inputs(seed: int = 0) -> dict:
    key_list = jax.random.split(jax.random.key(seed), 11)
    queries = draw_queries(jax.random.fold_in(key_list[10], 71), 0)
    key_states = draw_key_states(jax.random.fold_in(key_list[10], 71), 0)
    value_states = gaussian(key_list[2], (CLIPS, SRC, F), 1.0, 6.0, ((0, 32), (1, 8)))
    queries_dot = gaussian(key_list[3], (CLIPS, SRC, F), 1.0, 6.0, ((0, 32), (1, 8)))
    keys_dot = gaussian(key_list[4], (CLIPS, SRC, F), 1.0, 6.0, ((0, 32), (1, 8)))
    values_dot = gaussian(key_list[5], (CLIPS, SRC, F), 1.0, 6.0, ((0, 32), (1, 8)))
    velocity = gaussian(key_list[6], (CLIPS, SRC, D), 0.5, 3.0, ((0, 32), (1, 8)))
    time_gap = jnp.clip(0.3 + 0.7 * jax.random.uniform(key_list[7], (CLIPS,), jnp.float32) ** block_levels(key_list[7], (CLIPS,), ((0, 32),), -0.2, 0.2), 0.3, 1.0)
    merge_slot = draw_merge_slot(jax.random.fold_in(key_list[10], 71), 0)
    out_weight = gaussian(key_list[9], (D, F), F ** -0.5, 0.125, ((0, 256),))
    return dict(queries=queries, key_states=key_states, value_states=value_states, queries_dot=queries_dot, keys_dot=keys_dot, values_dot=values_dot, velocity=velocity, time_gap=time_gap, merge_slot=merge_slot, out_weight=out_weight)


def attend(queries, keys_in, values_in, queries_tan, keys_tan, values_tan):
    length = queries.shape[0]
    block = min(512, length)
    scale = 1.0 / math.sqrt(queries.shape[2])
    keys_f = keys_in.astype(jnp.float32)
    values_f = values_in.astype(jnp.float32)
    keys_tf = keys_tan.astype(jnp.float32)
    values_tf = values_tan.astype(jnp.float32)

    def one_block(index):
        start = index * block
        query_block = lax.dynamic_slice_in_dim(queries, start, block, 0).astype(jnp.float32)
        tangent_block = lax.dynamic_slice_in_dim(queries_tan, start, block, 0).astype(jnp.float32)
        scores = jnp.einsum('qhd,khd->hqk', query_block, keys_f) * scale
        scores_dot = (jnp.einsum('qhd,khd->hqk', tangent_block, keys_f) + jnp.einsum('qhd,khd->hqk', query_block, keys_tf)) * scale
        highest = lax.optimization_barrier(jnp.max(scores, axis=-1, keepdims=True))
        weights = jnp.exp(scores - highest)
        weights = weights / lax.optimization_barrier(jnp.sum(weights, axis=-1, keepdims=True))
        weights_dot = weights * (scores_dot - lax.optimization_barrier(jnp.sum(weights * scores_dot, axis=-1, keepdims=True)))
        probs = weights.astype(jnp.bfloat16).astype(jnp.float32)
        probs_dot = weights_dot.astype(jnp.bfloat16).astype(jnp.float32)
        mixed = jnp.einsum('hqk,khd->qhd', probs, values_f)
        mixed_dot = jnp.einsum('hqk,khd->qhd', probs_dot, values_f) + jnp.einsum('hqk,khd->qhd', probs, values_tf)
        return (mixed.astype(jnp.bfloat16), mixed_dot.astype(jnp.bfloat16))
    outputs = lax.map(one_block, jnp.arange(length // block, dtype=jnp.int32))
    return (outputs[0].reshape(queries.shape), outputs[1].reshape(queries.shape))

def reference(queries, key_states, value_states, queries_dot, keys_dot, values_dot, velocity, time_gap, merge_slot, out_weight):
    slots = jnp.arange(MERGED, dtype=jnp.int32)
    offsets = jnp.arange(SRC, dtype=jnp.int32) // SRC_DEV * MRG_DEV
    group_width = F // N_HEAD
    weight_groups = out_weight.astype(jnp.float32).reshape(D, N_HEAD, group_width)

    def project(data):
        grouped = data.astype(jnp.float32).reshape(MERGED, N_HEAD, group_width)
        parts = jnp.einsum('tgf,dgf->gtd', grouped, weight_groups, precision=lax.Precision.HIGHEST)
        parts = lax.optimization_barrier(parts.astype(jnp.bfloat16))
        return lax.optimization_barrier(jnp.sum(parts.astype(jnp.float32), axis=0)).astype(jnp.bfloat16)

    def one_clip(total, items):
        q_clip, k_clip, v_clip, tq_clip, tk_clip, tv_clip, vel_clip, gap_clip, slot_clip = items
        owner = slot_clip.astype(jnp.int32) + offsets
        select = owner[None, :] == slots[:, None]
        onehot = select.astype(jnp.bfloat16)
        counts = lax.optimization_barrier(jnp.sum(select.astype(jnp.float32), axis=1))

        def merge(data):
            summed = jnp.dot(onehot, data, preferred_element_type=jnp.float32)
            return (summed / counts[:, None]).astype(jnp.bfloat16).reshape(MERGED, HEADS, HD)
        merged = [merge(data) for data in (q_clip, k_clip, v_clip, tq_clip, tk_clip, tv_clip)]
        attn, attn_dot = attend(*merged)
        attn = attn.reshape(MERGED, F)
        attn_dot = attn_dot.reshape(MERGED, F)
        proj = project(attn)
        proj_dot = project(attn_dot)
        spread = onehot.T
        mean_flow = jnp.dot(spread, proj, preferred_element_type=jnp.float32)
        flow_dot = jnp.dot(spread, proj_dot, preferred_element_type=jnp.float32)
        residual = mean_flow - (vel_clip.astype(jnp.float32) - gap_clip * flow_dot)
        cotangent = jnp.dot(select.astype(jnp.float32), residual, precision=lax.Precision.HIGHEST).astype(jnp.bfloat16)
        grad_attn = jnp.dot(cotangent, out_weight, preferred_element_type=jnp.float32).astype(jnp.bfloat16)
        grad_term = jnp.dot(cotangent.T, attn, preferred_element_type=jnp.float32)
        return (total + grad_term, grad_attn)
    start_total = jnp.zeros((D, F), jnp.float32)
    total, grad_attn = lax.scan(one_clip, start_total, (queries, key_states, value_states, queries_dot, keys_dot, values_dot, velocity, time_gap, merge_slot))
    return (grad_attn, total)
```

```python
import math

import jax
import jax.numpy as jnp
from jax import lax
from jax.experimental import pallas as pl
from jax.experimental.pallas import tpu as pltpu
from jax.sharding import PartitionSpec as P

MESH = pl.DeviceIdType.MESH
HD = 128
GROUP = 256
TOK = 128
SRC_DEV = 256
MERGED = 1024
F = 2048
D = 3072
ROWS = 96
SCALE = 1.0 / math.sqrt(HD)

PEERS = ((0, 1), (1, 0), (1, 1), (3, 0), (3, 1), (2, 0), (2, 1))


def place():
    dp = lax.axis_index("dp")
    head = lax.axis_index("head")
    return dp // 16, (dp // 2) % 8, dp % 2, head // 4, head % 4


def dp_of(y_lo, z, core):
    return y_lo * 16 + z * 2 + core


def dot_t(a, b):
    return lax.dot_general(a, b, (((1,), (1,)), ((), ())), preferred_element_type=jnp.float32)


def front_kernel(
    q_hbm, k_hbm, tq_hbm, tk_hbm, v_hbm, tv_hbm, slot_ref, gap_ref, w_in,
    tok_ref, own_ref, w_out,
    stage, send, recv, send2, recv2, k2, v2, w_recv, w_own,
    in_sem, self_sem, a_send, a_recv, p_send, p_recv, w_send, w_rcv, w_self,
    y_send, y_recv, z_send, z_recv, s_send, s_recv,
):
    y_lo, z, core, y_hi, x = place()
    dp = lax.axis_index("dp")
    me = y_hi * 4 + x

    loads = []
    for i, ref in enumerate((q_hbm, k_hbm, tq_hbm, tk_hbm, v_hbm, tv_hbm)):
        load = pltpu.make_async_copy(ref, stage.at[i], in_sem.at[i])
        load.start()
        loads.append(load)

    def peer(r):
        dx, dy = PEERS[r]
        return ((y_hi + dy) % 2) * 4 + (x + dx) % 4

    peers = [peer(r) for r in range(7)]
    sibling = (dp_of(y_lo, z, 1 - core), me)
    partner = (dp_of(1 - y_lo, z, core), me)
    up = (dp_of(y_lo, (z + 1) % 8, core), me)
    down = (dp_of(y_lo, (z + 7) % 8, core), me)

    barrier = pltpu.get_barrier_semaphore()
    for p in peers:
        pl.semaphore_signal(barrier, inc=1, device_id=(dp, p), device_id_type=MESH)
    for who in (sibling, partner, up, down):
        pl.semaphore_signal(barrier, inc=1, device_id=who, device_id_type=MESH)
    pl.semaphore_wait(barrier, 11)

    def remote(src, dst, ssem, rsem, who):
        return pltpu.make_async_remote_copy(
            src_ref=src, dst_ref=dst, send_sem=ssem, recv_sem=rsem,
            device_id=who, device_id_type=MESH,
        )

    w_copies = []
    for r in range(7):
        copy = remote(w_in, w_recv.at[me], w_send.at[r], w_rcv.at[r], (dp, peers[r]))
        copy.start()
        w_copies.append(copy)
    w_local = pltpu.make_async_copy(w_in, w_recv.at[me], w_self.at[0])
    w_local.start()

    rows = lax.broadcasted_iota(jnp.int32, (TOK, SRC_DEV), 0)
    select = slot_ref[...] == rows
    counts = jnp.sum(select.astype(jnp.float32), axis=1, keepdims=True)
    inverse = 1.0 / counts
    onehot = select.astype(jnp.bfloat16)

    def merge(i):
        loads[i].wait()

        def body(h, carry):
            col = pl.multiple_of(h * GROUP, GROUP)
            total = jnp.dot(
                onehot, stage[i, :, pl.ds(col, GROUP)], preferred_element_type=jnp.float32
            )
            merged = (total * inverse).astype(jnp.bfloat16)
            send[h, 0, i] = merged[:, :HD]
            send[h, 1, i] = merged[:, HD:]
            return carry

        lax.fori_loop(0, 8, body, 0)

    def exchange(r, j, a):
        return remote(
            send.at[peers[r], j, pl.ds(3 * a, 3)],
            recv.at[j, me, pl.ds(3 * a, 3)],
            a_send.at[r, j, a],
            a_recv.at[r, j, a],
            (dp, peers[r]),
        )

    for i in range(3):
        merge(i)
    for r in range(7):
        exchange(r, 0, 0).start()
    for i in range(3, 6):
        merge(i)
    for j, a in ((0, 1), (1, 0), (1, 1)):
        for r in range(7):
            exchange(r, j, a).start()
    selfs = []
    for j in range(2):
        copy = pltpu.make_async_copy(send.at[me, j], recv.at[j, me], self_sem.at[j])
        copy.start()
        selfs.append(copy)

    for copy in w_copies:
        copy.wait()
    w_local.wait()
    out_row = lax.broadcasted_iota(jnp.int32, (ROWS, 128), 0)
    in_row = lax.broadcasted_iota(jnp.int32, (ROWS, 128), 1)
    pick = (in_row == (out_row // 12) * 16 + out_row % 12).astype(jnp.bfloat16)
    w_own[...] = jnp.dot(
        pick, w_recv[...].reshape(128, F), preferred_element_type=jnp.float32
    ).astype(jnp.bfloat16)

    def slot(b, plane):
        held = y_lo if b == 0 else 1 - y_lo
        return w_out.at[held * 8 + plane, core]

    pending = []

    def ring(way, step, b, src, plane):
        copy = remote(
            src, slot(b, plane), z_send.at[way, step, b], z_recv.at[way, step, b],
            up if way == 0 else down,
        )
        copy.start()
        pending.append(copy)

    def landed(way, step, b):
        plane = (z + (8 - step if way == 0 else step)) % 8
        ref = slot(b, plane)
        remote(
            ref, ref, z_send.at[way, step - 1, b], z_recv.at[way, step - 1, b],
            up if way == 0 else down,
        ).wait_recv()
        return ref, plane

    across = []

    def to_sibling(src, dst):
        n = len(across)
        copy = remote(src, dst, s_send.at[n], s_recv.at[n], sibling)
        copy.start()
        across.append(copy)

    own_slot = slot(0, z)
    ring(0, 0, 0, w_own, z)
    ring(1, 0, 0, w_own, z)
    to_partner = remote(w_own, own_slot, y_send.at[0], y_recv.at[0], partner)
    to_partner.start()
    to_sibling(w_own, own_slot)
    keep = pltpu.make_async_copy(w_own, own_slot, w_self.at[1])
    keep.start()
    other = slot(1, z)
    remote(other, other, y_send.at[0], y_recv.at[0], partner).wait_recv()
    ring(0, 0, 1, other, z)
    ring(1, 0, 1, other, z)
    to_sibling(other, other)

    def ring_step(step, b):
        for way in range(2):
            if step == 4 and way != b:
                continue
            ref, plane = landed(way, step, b)
            if step < 3 or (step == 3 and way == b):
                ring(way, step, b, ref, plane)
            to_sibling(ref, ref)

    gap = gap_ref[0, 0]

    def attend(j):
        for a in range(2):
            for r in range(7):
                exchange(r, j, a).wait_recv()
        selfs[j].wait()
        for t in range(8):
            here = pl.ds(t * TOK, TOK)
            k2[here, :HD] = recv[j, t, 1]
            k2[here, HD:] = recv[j, t, 3]
            v2[here, :HD] = recv[j, t, 4]
            v2[here, HD:] = recv[j, t, 5]

        def block(n, carry):
            q = recv[j, pl.ds(2 * n, 2), 0].reshape(2 * TOK, HD)
            tq = recv[j, pl.ds(2 * n, 2), 2].reshape(2 * TOK, HD)
            scores = dot_t(q, k2[:, :HD])
            scores_dot = dot_t(jnp.concatenate([tq, q], axis=1), k2[...])
            highest = jnp.max(scores, axis=1, keepdims=True)
            weights = jnp.exp((scores - highest) * SCALE)
            total = jnp.sum(weights, axis=1, keepdims=True)
            mean = jnp.sum(weights * scores_dot, axis=1, keepdims=True) / total
            tangent = (weights * (scores_dot - mean)).astype(jnp.bfloat16)
            mixed = jnp.dot(
                weights.astype(jnp.bfloat16), v2[...], preferred_element_type=jnp.float32
            )
            moved = jnp.dot(tangent, v2[:, :HD], preferred_element_type=jnp.float32)
            norm = 1.0 / total
            attn = mixed[:, :HD] * norm
            attn_dot = (moved * SCALE + mixed[:, HD:]) * norm
            both = (attn + gap * attn_dot).astype(jnp.bfloat16)
            start = pl.multiple_of(n * 2 * TOK, 2 * TOK)
            own_ref[pl.ds(start, 2 * TOK), j * HD : (j + 1) * HD] = attn.astype(jnp.bfloat16)
            send2[j, pl.ds(2 * n, 2)] = both.reshape(2, TOK, HD)
            return carry

        lax.fori_loop(0, 4, block, 0)

    def back(r, j):
        return remote(
            send2.at[j, peers[r]], recv2.at[j, me], p_send.at[r, j], p_recv.at[r, j],
            (dp, peers[r]),
        )

    ring_step(1, 0)
    ring_step(1, 1)
    attend(0)
    for r in range(7):
        back(r, 0).start()
    ring_step(2, 0)
    ring_step(2, 1)
    attend(1)
    for r in range(7):
        back(r, 1).start()
    recv2[:, pl.ds(me, 1)] = send2[:, pl.ds(me, 1)]
    ring_step(3, 0)
    for j in range(2):
        for r in range(7):
            back(r, j).wait_recv()
    for j in range(2):
        for h in range(8):
            col = h * GROUP + j * HD
            tok_ref[:, col : col + HD] = recv2[j, h]
    ring_step(3, 1)
    ring_step(4, 0)
    ring_step(4, 1)

    keep.wait()
    to_partner.wait_send()
    for copy in pending:
        copy.wait_send()
    for copy in across:
        copy.wait()
    for r in range(7):
        for j in range(2):
            back(r, j).wait_send()
            for a in range(2):
                exchange(r, j, a).wait_send()


def front(queries, key_states, queries_dot, keys_dot, value_states, values_dot, slot, gap, w_in):
    any_spec = pl.BlockSpec(memory_space=pl.ANY)
    vmem = pl.BlockSpec(memory_space=pltpu.VMEM)
    bf = jnp.bfloat16
    dma = pltpu.SemaphoreType.DMA
    return pl.pallas_call(
        front_kernel,
        out_shape=(
            jax.ShapeDtypeStruct((TOK, F), bf),
            jax.ShapeDtypeStruct((MERGED, GROUP), bf),
            jax.ShapeDtypeStruct((16, 2, ROWS, F), bf),
        ),
        in_specs=[any_spec] * 6 + [vmem, pl.BlockSpec(memory_space=pltpu.SMEM), vmem],
        out_specs=(vmem, vmem, any_spec),
        scratch_shapes=[
            pltpu.VMEM((6, SRC_DEV, F), bf),
            pltpu.VMEM((8, 2, 6, TOK, HD), bf),
            pltpu.VMEM((2, 8, 6, TOK, HD), bf),
            pltpu.VMEM((2, 8, TOK, HD), bf),
            pltpu.VMEM((2, 8, TOK, HD), bf),
            pltpu.VMEM((MERGED, 2 * HD), bf),
            pltpu.VMEM((MERGED, 2 * HD), bf),
            pltpu.VMEM((8, 16, F), bf),
            pltpu.VMEM((ROWS, F), bf),
            dma((6,)),
            dma((2,)),
            dma((7, 2, 2)),
            dma((7, 2, 2)),
            dma((7, 2)),
            dma((7, 2)),
            dma((7,)),
            dma((7,)),
            dma((2,)),
            dma((1,)),
            dma((1,)),
            dma((2, 4, 2)),
            dma((2, 4, 2)),
            dma((16,)),
            dma((16,)),
        ],
        compiler_params=pltpu.CompilerParams(
            collective_id=0, has_side_effects=True, vmem_limit_bytes=44 << 20
        ),
        cost_estimate=pl.CostEstimate(
            flops=5_000_000_000, bytes_accessed=32 << 20, transcendentals=2 << 20
        ),
    )(queries, key_states, queries_dot, keys_dot, value_states, values_dot, slot, gap, w_in)


def on_device(
    queries, key_states, value_states, queries_dot, keys_dot, values_dot,
    velocity, time_gap, merge_slot, out_weight,
):
    select = merge_slot[0][None, :] == jnp.arange(TOK, dtype=jnp.int32)[:, None]
    onehot = select.astype(jnp.bfloat16)
    counts = jnp.sum(select.astype(jnp.float32), axis=1)
    moved = jnp.dot(onehot, velocity[0], preferred_element_type=jnp.float32)
    attn_tok, attn_own, weights = front(
        queries[0], key_states[0], queries_dot[0], keys_dot[0], value_states[0], values_dot[0],
        merge_slot, time_gap.reshape(1, 1), jnp.pad(out_weight, ((0, 4), (0, 0))),
    )
    full_weight = weights.reshape(D, F)
    proj = dot_t(attn_tok, full_weight)
    cotangent = (counts[:, None] * proj - moved).astype(jnp.bfloat16)
    head_weight = lax.dynamic_slice_in_dim(
        full_weight, lax.axis_index("head") * GROUP, GROUP, 1
    )
    clip_cotangent = lax.all_gather(cotangent, "head", axis=0, tiled=True)
    grad_attn = jnp.dot(
        clip_cotangent, head_weight, preferred_element_type=jnp.float32
    ).astype(jnp.bfloat16)
    grad_weight = lax.psum_scatter(
        lax.dot_general(
            clip_cotangent, attn_own, (((0,), (0,)), ((), ())), preferred_element_type=jnp.float32
        ),
        "dp",
        scatter_dimension=0,
        tiled=True,
    )
    return (grad_attn[None], grad_weight)


def solution(mesh):
    block = P("dp", "head", None)
    return jax.shard_map(
        on_device,
        mesh=mesh,
        in_specs=(block,) * 7 + (P("dp"), P("dp", "head"), P(("dp", "head"), None)),
        out_specs=(P("dp", None, "head"), P("dp", "head")),
        check_vma=False,
    )
```

```python
import math

import jax
import jax.numpy as jnp
from jax import lax
from jax.experimental import pallas as pl
from jax.experimental.pallas import tpu as pltpu
from jax.sharding import PartitionSpec as P

MESH = pl.DeviceIdType.MESH
HD = 128
GROUP = 256
TOK = 128
SRC_DEV = 256
MERGED = 1024
F = 2048
D = 3072
ROWS = 96
SCALE = 1.0 / math.sqrt(HD)

PEERS = ((0, 1), (1, 0), (1, 1), (3, 0), (3, 1), (2, 0), (2, 1))


def place():
    dp = lax.axis_index("dp")
    head = lax.axis_index("head")
    return dp // 16, (dp // 2) % 8, dp % 2, head // 4, head % 4


def dp_of(y_lo, z, core):
    return y_lo * 16 + z * 2 + core


def dot_t(a, b):
    return lax.dot_general(a, b, (((1,), (1,)), ((), ())), preferred_element_type=jnp.float32)


def clip_kernel(
    q_hbm, k_hbm, tq_hbm, tk_hbm, v_hbm, tv_hbm, vel_hbm, slot_ref, gap_ref, w_in,
    ga_ref, gw_ref,
    stage, vel, send, recv, send2, own, k2, v2, w_recv, w_own, w_all, tok, full, acc,
    c_send_buf, quarter, g_buf, term, term_sib, rs_buf, rs_recv, fin,
    in_sem, self_sem, a_send, a_recv, p_send, p_recv, f_send, f_recv, w_send, w_rcv, w_self,
    y_send, y_recv, z_send, z_recv, s_send, s_recv, c_send, c_recv, g_send, g_recv,
    b_send, b_recv, r_send, r_recv, e_send, e_recv,
):
    y_lo, z, core, y_hi, x = place()
    dp = lax.axis_index("dp")
    me = y_hi * 4 + x

    loads = []
    for i, ref in enumerate((q_hbm, k_hbm, tq_hbm, tk_hbm, v_hbm, tv_hbm)):
        load = pltpu.make_async_copy(ref, stage.at[i], in_sem.at[i])
        load.start()
        loads.append(load)
    vel_load = pltpu.make_async_copy(vel_hbm, vel, in_sem.at[6])
    vel_load.start()

    peers = [((y_hi + dy) % 2) * 4 + (x + dx) % 4 for dx, dy in PEERS]
    sibling = (dp_of(y_lo, z, 1 - core), me)
    partner = (dp_of(1 - y_lo, z, core), me)
    up = (dp_of(y_lo, (z + 1) % 8, core), me)
    down = (dp_of(y_lo, (z + 7) % 8, core), me)

    turn = (z + 7) % 8
    dest_x = turn % 4
    dest_z = 4 * (x % 2) + 2 * ((y_lo + dest_x + 1) % 2) + turn // 4
    dest = (dp_of(x // 2, dest_z, core), y_hi * 4 + dest_x)
    from_x = 2 * y_lo + z // 4
    from_z = (((z % 4) % 2) * 4 + x + 1) % 8
    source = (dp_of(((z % 4) // 2 + x + 1) % 2, from_z, core), y_hi * 4 + from_x)

    barrier = pltpu.get_barrier_semaphore()

    def greet(who):
        pl.semaphore_signal(barrier, inc=1, device_id=who, device_id_type=MESH)

    for p in peers:
        greet((dp, p))
    for dy in range(2):
        for dz in range(8):
            if dy or dz:
                greet((dp_of((y_lo + dy) % 2, (z + dz) % 8, core), me))
    greet(sibling)
    greet(dest)
    greet(source)
    pl.semaphore_wait(barrier, 25)

    def remote(src, dst, ssem, rsem, who):
        return pltpu.make_async_remote_copy(
            src_ref=src, dst_ref=dst, send_sem=ssem, recv_sem=rsem,
            device_id=who, device_id_type=MESH,
        )

    w_copies = []
    for r in range(7):
        copy = remote(w_in, w_recv.at[me], w_send.at[r], w_rcv.at[r], (dp, peers[r]))
        copy.start()
        w_copies.append(copy)
    w_local = pltpu.make_async_copy(w_in, w_recv.at[me], w_self.at[0])
    w_local.start()

    rows = lax.broadcasted_iota(jnp.int32, (TOK, SRC_DEV), 0)
    select = slot_ref[...] == rows
    counts = jnp.sum(select.astype(jnp.float32), axis=1, keepdims=True)
    inverse = 1.0 / counts
    onehot = select.astype(jnp.bfloat16)

    def merge(i):
        loads[i].wait()

        def body(h, carry):
            col = pl.multiple_of(h * GROUP, GROUP)
            total = jnp.dot(
                onehot, stage[i, :, pl.ds(col, GROUP)], preferred_element_type=jnp.float32
            )
            merged = (total * inverse).astype(jnp.bfloat16)
            send[h, 0, i] = merged[:, :HD]
            send[h, 1, i] = merged[:, HD:]
            return carry

        lax.fori_loop(0, 8, body, 0)

    def exchange(r, j, a):
        return remote(
            send.at[peers[r], j, pl.ds(3 * a, 3)],
            recv.at[j, me, pl.ds(3 * a, 3)],
            a_send.at[r, j, a],
            a_recv.at[r, j, a],
            (dp, peers[r]),
        )

    for i in range(3):
        merge(i)

    for copy in w_copies:
        copy.wait()
    w_local.wait()
    out_row = lax.broadcasted_iota(jnp.int32, (ROWS, 128), 0)
    in_row = lax.broadcasted_iota(jnp.int32, (ROWS, 128), 1)
    pick = (in_row == (out_row // 12) * 16 + out_row % 12).astype(jnp.bfloat16)
    w_own[...] = jnp.dot(
        pick, w_recv[...].reshape(128, F), preferred_element_type=jnp.float32
    ).astype(jnp.bfloat16)

    def slot(b, plane):
        held = y_lo if b == 0 else 1 - y_lo
        first = pl.multiple_of(dp_of(held, plane, core) * ROWS, ROWS)
        return w_all.at[pl.ds(first, ROWS)]

    pending = []

    def ring(way, step, b, src, plane):
        copy = remote(
            src, slot(b, plane), z_send.at[way, step, b], z_recv.at[way, step, b],
            up if way == 0 else down,
        )
        copy.start()
        pending.append(copy)

    def landed(way, step, b):
        plane = (z + (8 - step if way == 0 else step)) % 8
        ref = slot(b, plane)
        remote(
            ref, ref, z_send.at[way, step - 1, b], z_recv.at[way, step - 1, b],
            up if way == 0 else down,
        ).wait_recv()
        return ref, plane

    across = []

    def to_sibling(src, dst):
        n = len(across)
        copy = remote(src, dst, s_send.at[n], s_recv.at[n], sibling)
        copy.start()
        across.append(copy)

    taken = [0]

    def from_sibling(upto):
        for n in range(taken[0], upto):
            across[n].wait_recv()
        taken[0] = upto

    own_slot = slot(0, z)
    to_partner = remote(w_own, own_slot, y_send.at[0], y_recv.at[0], partner)
    to_partner.start()
    ring(0, 0, 0, w_own, z)
    ring(1, 0, 0, w_own, z)
    to_sibling(w_own, own_slot)
    keep = pltpu.make_async_copy(w_own, own_slot, w_self.at[1])
    keep.start()

    for r in range(7):
        exchange(r, 0, 0).start()
    for i in range(3, 6):
        merge(i)
    for j, a in ((0, 1), (1, 0), (1, 1)):
        for r in range(7):
            exchange(r, j, a).start()
    selfs = []
    for j in range(2):
        copy = pltpu.make_async_copy(send.at[me, j], recv.at[j, me], self_sem.at[j])
        copy.start()
        selfs.append(copy)

    other = slot(1, z)
    remote(other, other, y_send.at[0], y_recv.at[0], partner).wait_recv()
    ring(0, 0, 1, other, z)
    ring(1, 0, 1, other, z)
    to_sibling(other, other)

    def ring_step(step, b):
        for way in range(2):
            if step == 4 and way != b:
                continue
            ref, plane = landed(way, step, b)
            if step < 3 or (step == 3 and way == b):
                ring(way, step, b, ref, plane)
            to_sibling(ref, ref)

    gap = gap_ref[0, 0]

    def attend(j):
        for a in range(2):
            for r in range(7):
                exchange(r, j, a).wait_recv()
        selfs[j].wait()
        for t in range(8):
            here = pl.ds(t * TOK, TOK)
            k2[here, :HD] = recv[j, t, 1]
            k2[here, HD:] = recv[j, t, 3]
            v2[here, :HD] = recv[j, t, 4]
            v2[here, HD:] = recv[j, t, 5]

        def block(n, carry):
            q = recv[j, pl.ds(2 * n, 2), 0].reshape(2 * TOK, HD)
            tq = recv[j, pl.ds(2 * n, 2), 2].reshape(2 * TOK, HD)
            scores = dot_t(q, k2[:, :HD])
            scores_dot = dot_t(jnp.concatenate([tq, q], axis=1), k2[...])
            highest = jnp.max(scores, axis=1, keepdims=True)
            weights = jnp.exp((scores - highest) * SCALE)
            total = jnp.sum(weights, axis=1, keepdims=True)
            mean = jnp.sum(weights * scores_dot, axis=1, keepdims=True) / total
            tangent = (weights * (scores_dot - mean)).astype(jnp.bfloat16)
            mixed = jnp.dot(
                weights.astype(jnp.bfloat16), v2[...], preferred_element_type=jnp.float32
            )
            moved = jnp.dot(tangent, v2[:, :HD], preferred_element_type=jnp.float32)
            norm = 1.0 / total
            attn = mixed[:, :HD] * norm
            attn_dot = (moved * SCALE + mixed[:, HD:]) * norm
            both = (attn + gap * attn_dot).astype(jnp.bfloat16)
            start = pl.multiple_of(n * 2 * TOK, 2 * TOK)
            own[j, pl.ds(start, 2 * TOK)] = attn.astype(jnp.bfloat16)
            send2[j, pl.ds(2 * n, 2)] = both.reshape(2, TOK, HD)
            return carry

        lax.fori_loop(0, 4, block, 0)

    def back(r, j):
        col = pl.multiple_of(me * GROUP + j * HD, HD)
        return remote(
            send2.at[j, peers[r]], tok.at[:, pl.ds(col, HD)], p_send.at[r, j], p_recv.at[r, j],
            (dp, peers[r]),
        )

    def along(dx, j):
        col = pl.multiple_of(x * GROUP + j * HD, HD)
        return remote(
            own.at[j], full.at[:, pl.ds(col, HD)], f_send.at[dx - 1, j], f_recv.at[dx - 1, j],
            (dp, y_hi * 4 + (x + dx) % 4),
        )

    locals_ = []

    def hand_out(j):
        for r in range(7):
            back(r, j).start()
        for dx in (1, 3, 2):
            along(dx, j).start()
        col = pl.multiple_of(me * GROUP + j * HD, HD)
        copy = pltpu.make_async_copy(send2.at[j, me], tok.at[:, pl.ds(col, HD)], self_sem.at[2 + j])
        copy.start()
        locals_.append(copy)
        col = pl.multiple_of(x * GROUP + j * HD, HD)
        copy = pltpu.make_async_copy(own.at[j], full.at[:, pl.ds(col, HD)], self_sem.at[4 + j])
        copy.start()
        locals_.append(copy)

    ring_step(1, 0)
    ring_step(1, 1)
    attend(0)
    hand_out(0)
    ring_step(2, 0)
    ring_step(2, 1)
    attend(1)
    hand_out(1)
    vel_load.wait()
    for j in range(2):
        for r in range(7):
            back(r, j).wait_recv()
    for copy in locals_:
        copy.wait()
    keep.wait()

    near = z // 2
    side = 1 - 2 * (z % 2)
    pairs = (near, (near + 4 - side) % 4, (near + side) % 4, (near + 2) % 4)

    def quarter_copy(n, lo, way):
        pair = pairs[n]
        to = 2 * lo + pair // 2
        half = pair % 2
        col = pl.multiple_of(me * TOK, TOK)
        y_to = (y_hi + way) % 2
        return remote(
            c_send_buf.at[n, lo], quarter.at[half, :, pl.ds(col, TOK)],
            c_send.at[n, lo, way], c_recv.at[half, way * 4 + (to + 4 - x) % 4],
            (dp, y_to * 4 + to),
        )

    def local_quarter(n, lo):
        half = pairs[n] % 2
        col = pl.multiple_of(me * TOK, TOK)
        return pltpu.make_async_copy(
            c_send_buf.at[n, lo], quarter.at[half, :, pl.ds(col, TOK)], self_sem.at[6 + half]
        )

    def project(n):
        pair = pairs[n]
        for lo in range(2):
            first = pl.multiple_of(lo * 1536 + pair * 384, 384)
            weights = w_all[pl.ds(first, 384)]
            proj = dot_t(tok[...], weights)
            moved = jnp.dot(
                onehot, vel[:, pl.ds(first, 384)], preferred_element_type=jnp.float32
            )
            cot = counts * proj - moved
            c_send_buf[n, lo] = cot.T.astype(jnp.bfloat16)
            to = 2 * lo + pair // 2
            quarter_copy(n, lo, 1).start()

            @pl.when(to != x)
            def _():
                quarter_copy(n, lo, 0).start()

            @pl.when(to == x)
            def _():
                local_quarter(n, lo).start()

            part = jnp.dot(cot.astype(jnp.bfloat16), weights, preferred_element_type=jnp.float32)
            if n == 0 and lo == 0:
                acc[...] = part
            else:
                acc[...] += part

    from_sibling(6)
    project(0)
    from_sibling(10)
    project(1)
    ring_step(3, 0)
    ring_step(3, 1)
    from_sibling(14)
    project(2)
    ring_step(4, 0)
    ring_step(4, 1)
    from_sibling(16)
    project(3)

    def grads(r):
        here = pl.ds(pl.multiple_of(me * TOK, TOK), TOK)
        return remote(
            g_buf.at[peers[r]], ga_ref.at[here], g_send.at[r], g_recv.at[r], (dp, peers[r])
        )

    for h in range(8):
        g_buf[h] = acc[:, h * GROUP : (h + 1) * GROUP].astype(jnp.bfloat16)
    for r in range(7):
        grads(r).start()
    ga_own = pltpu.make_async_copy(
        g_buf.at[me], ga_ref.at[pl.ds(pl.multiple_of(me * TOK, TOK), TOK)], self_sem.at[8]
    )
    ga_own.start()

    early = (near % 2 + (near // 2 + x) % 2) % 2
    halves = (early, 1 - early)

    def half_term(half):
        for way in range(2):
            for dx in range(4):
                if way or dx:
                    col = pl.multiple_of(me * TOK, TOK)
                    remote(
                        c_send_buf.at[0, 0], quarter.at[half, :, pl.ds(col, TOK)],
                        c_send.at[0, 0, 0], c_recv.at[half, way * 4 + dx], sibling,
                    ).wait_recv()
        pltpu.make_async_copy(
            c_send_buf.at[0, 0], quarter.at[half, :, pl.ds(0, TOK)], self_sem.at[6 + half]
        ).wait()
        for block in range(4):
            part = jnp.dot(
                quarter[half], full[:, block * GROUP : (block + 1) * GROUP],
                preferred_element_type=jnp.float32,
            )
            for zi in range(2):
                for c in range(2):
                    top = zi * 192 + c * ROWS
                    term[half, c, zi, block] = part[top : top + ROWS]
        copy = swap(half)
        copy.start()

    def swap(half):
        return remote(
            term.at[half, 1 - core], term_sib.at[half], b_send.at[half], b_recv.at[half], sibling
        )

    def reduce_copy(half, dz):
        turn_to = (z + dz + 7) % 8
        zi = turn_to // 4
        block = turn_to % 4
        lo = (half + block + 1) % 2
        rel = ((lo + y_lo) % 2) * 8 + dz
        return lo, zi, block, remote(
            rs_buf.at[half, zi, block], rs_recv.at[rel], r_send.at[half, dz], r_recv.at[rel],
            (dp_of(lo, (z + dz) % 8, core), me),
        )

    def spread(half):
        swap(half).wait_recv()
        for dz in (4, 3, 5, 2, 6, 1, 7, 0):
            lo, zi, block, copy = reduce_copy(half, dz)
            rs_buf[half, zi, block] = (
                term[half, core, zi, block] + term_sib[half, zi, block]
            ).astype(jnp.bfloat16)
            if dz:
                copy.start()
            else:

                @pl.when(lo != y_lo)
                def _():
                    copy.start()

                @pl.when(lo == y_lo)
                def _():
                    rs_recv[0] = rs_buf[half, zi, block]

    for dx in (1, 3, 2):
        for j in range(2):
            along(dx, j).wait_recv()
    for half in halves:
        half_term(half)
    for half in halves:
        spread(half)

    for rel in range(1, 16):
        remote(
            rs_buf.at[0, 0, 0], rs_recv.at[rel], r_send.at[0, 0], r_recv.at[rel], sibling
        ).wait_recv()

    def add(rel, total):
        return total + rs_recv[rel].astype(jnp.float32)

    fin[...] = lax.fori_loop(0, 16, add, jnp.zeros((ROWS, GROUP), jnp.float32))
    place_copy = remote(fin, gw_ref, e_send.at[0], e_recv.at[0], dest)
    place_copy.start()

    to_partner.wait_send()
    for copy in pending:
        copy.wait_send()
    for copy in across:
        copy.wait_send()
    for r in range(7):
        for j in range(2):
            back(r, j).wait_send()
            for a in range(2):
                exchange(r, j, a).wait_send()
        grads(r).wait()
    ga_own.wait()
    for dx in (1, 3, 2):
        for j in range(2):
            along(dx, j).wait_send()
    for n in range(4):
        for lo in range(2):
            quarter_copy(n, lo, 1).wait_send()

            @pl.when(2 * lo + pairs[n] // 2 != x)
            def _():
                quarter_copy(n, lo, 0).wait_send()

    for half in range(2):
        swap(half).wait_send()
        for dz in range(8):
            lo, _, _, copy = reduce_copy(half, dz)
            if dz:
                copy.wait_send()
            else:

                @pl.when(lo != y_lo)
                def _():
                    copy.wait_send()

    place_copy.wait()


def clip_call(queries, key_states, queries_dot, keys_dot, value_states, values_dot, velocity, slot, gap, w_in):
    any_spec = pl.BlockSpec(memory_space=pl.ANY)
    vmem = pl.BlockSpec(memory_space=pltpu.VMEM)
    bf = jnp.bfloat16
    f32 = jnp.float32
    dma = pltpu.SemaphoreType.DMA
    return pl.pallas_call(
        clip_kernel,
        out_shape=(
            jax.ShapeDtypeStruct((MERGED, GROUP), bf),
            jax.ShapeDtypeStruct((ROWS, GROUP), f32),
        ),
        in_specs=[any_spec] * 7 + [vmem, pl.BlockSpec(memory_space=pltpu.SMEM), vmem],
        out_specs=(vmem, vmem),
        scratch_shapes=[
            pltpu.VMEM((6, SRC_DEV, F), bf),
            pltpu.VMEM((SRC_DEV, D), bf),
            pltpu.VMEM((8, 2, 6, TOK, HD), bf),
            pltpu.VMEM((2, 8, 6, TOK, HD), bf),
            pltpu.VMEM((2, 8, TOK, HD), bf),
            pltpu.VMEM((2, MERGED, HD), bf),
            pltpu.VMEM((MERGED, 2 * HD), bf),
            pltpu.VMEM((MERGED, 2 * HD), bf),
            pltpu.VMEM((8, 16, F), bf),
            pltpu.VMEM((ROWS, F), bf),
            pltpu.VMEM((D, F), bf),
            pltpu.VMEM((TOK, F), bf),
            pltpu.VMEM((MERGED, 4 * GROUP), bf),
            pltpu.VMEM((TOK, F), f32),
            pltpu.VMEM((4, 2, 384, TOK), bf),
            pltpu.VMEM((2, 384, MERGED), bf),
            pltpu.VMEM((8, TOK, GROUP), bf),
            pltpu.VMEM((2, 2, 2, 4, ROWS, GROUP), f32),
            pltpu.VMEM((2, 2, 4, ROWS, GROUP), f32),
            pltpu.VMEM((2, 2, 4, ROWS, GROUP), bf),
            pltpu.VMEM((16, ROWS, GROUP), bf),
            pltpu.VMEM((ROWS, GROUP), f32),
            dma((7,)),
            dma((9,)),
            dma((7, 2, 2)),
            dma((7, 2, 2)),
            dma((7, 2)),
            dma((7, 2)),
            dma((3, 2)),
            dma((3, 2)),
            dma((7,)),
            dma((7,)),
            dma((2,)),
            dma((1,)),
            dma((1,)),
            dma((2, 4, 2)),
            dma((2, 4, 2)),
            dma((16,)),
            dma((16,)),
            dma((4, 2, 2)),
            dma((2, 8)),
            dma((7,)),
            dma((7,)),
            dma((2,)),
            dma((2,)),
            dma((2, 8)),
            dma((16,)),
            dma((1,)),
            dma((1,)),
        ],
        compiler_params=pltpu.CompilerParams(
            collective_id=0, has_side_effects=True, vmem_limit_bytes=60 << 20
        ),
        cost_estimate=pl.CostEstimate(
            flops=10_000_000_000, bytes_accessed=9 << 20, transcendentals=2 << 20
        ),
    )(
        queries, key_states, queries_dot, keys_dot, value_states, values_dot, velocity,
        slot, gap, w_in,
    )


def on_device(
    queries, key_states, value_states, queries_dot, keys_dot, values_dot,
    velocity, time_gap, merge_slot, out_weight,
):
    grad_attn, grad_weight = clip_call(
        queries[0], key_states[0], queries_dot[0], keys_dot[0], value_states[0], values_dot[0],
        velocity[0], merge_slot, time_gap.reshape(1, 1), jnp.pad(out_weight, ((0, 4), (0, 0))),
    )
    return (grad_attn[None], grad_weight)


def solution(mesh):
    block = P("dp", "head", None)
    return jax.shard_map(
        on_device,
        mesh=mesh,
        in_specs=(block,) * 7 + (P("dp"), P("dp", "head"), P(("dp", "head"), None)),
        out_specs=(P("dp", None, "head"), P("dp", "head")),
        check_vma=False,
    )
```

```python
import math

import jax
import jax.numpy as jnp
from jax import lax
from jax.experimental import pallas as pl
from jax.experimental.pallas import tpu as pltpu
from jax.sharding import PartitionSpec as P

MESH = pl.DeviceIdType.MESH
HD = 128
GROUP = 256
TOK = 128
SRC_DEV = 256
MERGED = 1024
F = 2048
D = 3072
ROWS = 96
SCALE = 1.0 / math.sqrt(HD)

PEERS = ((0, 1), (1, 0), (1, 1), (3, 0), (3, 1), (2, 0), (2, 1))


def place():
    dp = lax.axis_index("dp")
    head = lax.axis_index("head")
    return dp // 16, (dp // 2) % 8, dp % 2, head // 4, head % 4


def dp_of(y_lo, z, core):
    return y_lo * 16 + z * 2 + core


def dot_t(a, b):
    return lax.dot_general(a, b, (((1,), (1,)), ((), ())), preferred_element_type=jnp.float32)


def clip_kernel(
    q_hbm, k_hbm, tq_hbm, tk_hbm, v_hbm, tv_hbm, vel_hbm, slot_ref, gap_ref, w_in,
    ga_ref, gw_ref,
    w_pad, stage, vel, send, recv, send2, own, k2, v2, w_recv, w_own, w_all, tok, full, acc,
    c_send_buf, quarter, g_buf, term, term_sib, rs_buf, rs_recv, fin,
    in_sem, self_sem, a_send, a_recv, p_send, p_recv, f_send, f_recv, w_send, w_rcv, w_self,
    y_send, y_recv, z_send, z_recv, s_send, s_recv, c_send, c_recv, g_send, g_recv,
    b_send, b_recv, r_send, r_recv, e_send, e_recv,
):
    y_lo, z, core, y_hi, x = place()
    dp = lax.axis_index("dp")
    me = y_hi * 4 + x

    peers = [((y_hi + dy) % 2) * 4 + (x + dx) % 4 for dx, dy in PEERS]
    sibling = (dp_of(y_lo, z, 1 - core), me)
    partner = (dp_of(1 - y_lo, z, core), me)
    up = (dp_of(y_lo, (z + 1) % 8, core), me)
    down = (dp_of(y_lo, (z + 7) % 8, core), me)

    turn = (z + 7) % 8
    dest_x = turn % 4
    dest_z = 4 * (x % 2) + 2 * ((y_lo + dest_x + 1) % 2) + turn // 4
    dest = (dp_of(x // 2, dest_z, core), y_hi * 4 + dest_x)
    from_x = 2 * y_lo + z // 4
    from_z = (((z % 4) % 2) * 4 + x + 1) % 8
    source = (dp_of(((z % 4) // 2 + x + 1) % 2, from_z, core), y_hi * 4 + from_x)

    barrier = pltpu.get_barrier_semaphore()

    def greet(who):
        pl.semaphore_signal(barrier, inc=1, device_id=who, device_id_type=MESH)

    for p in peers:
        greet((dp, p))
    for dy in range(2):
        for dz in range(8):
            if dy or dz:
                greet((dp_of((y_lo + dy) % 2, (z + dz) % 8, core), me))
    greet(sibling)
    greet(dest)
    greet(source)

    loads = []
    for i, ref in enumerate((q_hbm, k_hbm, tq_hbm, tk_hbm, v_hbm, tv_hbm)):
        load = pltpu.make_async_copy(ref, stage.at[i], in_sem.at[i])
        load.start()
        loads.append(load)
    vel_load = pltpu.make_async_copy(vel_hbm, vel, in_sem.at[6])
    vel_load.start()
    w_pad[...] = jnp.zeros_like(w_pad)
    w_pad[:12] = w_in[...]

    def remote(src, dst, ssem, rsem, who):
        return pltpu.make_async_remote_copy(
            src_ref=src, dst_ref=dst, send_sem=ssem, recv_sem=rsem,
            device_id=who, device_id_type=MESH,
        )

    rows = lax.broadcasted_iota(jnp.int32, (TOK, SRC_DEV), 0)
    select = slot_ref[...] == rows
    counts = jnp.sum(select.astype(jnp.float32), axis=1, keepdims=True)
    inverse = 1.0 / counts
    onehot = select.astype(jnp.bfloat16)

    def merge(i):
        loads[i].wait()

        def body(n, carry):
            col = pl.multiple_of(n * 4 * GROUP, 4 * GROUP)
            total = jnp.dot(
                onehot, stage[i, :, pl.ds(col, 4 * GROUP)], preferred_element_type=jnp.float32
            )
            merged = (total * inverse).astype(jnp.bfloat16)
            for h in range(4):
                for j in range(2):
                    first = h * GROUP + j * HD
                    send[4 * n + h, j, i] = merged[:, first : first + HD]
            return carry

        lax.fori_loop(0, 2, body, 0)

    def exchange(r, j, a):
        return remote(
            send.at[peers[r], j, pl.ds(3 * a, 3)],
            recv.at[j, me, pl.ds(3 * a, 3)],
            a_send.at[r, j, a],
            a_recv.at[r, j, a],
            (dp, peers[r]),
        )

    for i in range(6):
        merge(i)
    pl.semaphore_wait(barrier, 25)

    w_copies = []
    for r in range(7):
        copy = remote(w_pad, w_recv.at[me], w_send.at[r], w_rcv.at[r], (dp, peers[r]))
        copy.start()
        w_copies.append(copy)
    w_local = pltpu.make_async_copy(w_pad, w_recv.at[me], w_self.at[0])
    w_local.start()

    for copy in w_copies:
        copy.wait()
    w_local.wait()
    out_row = lax.broadcasted_iota(jnp.int32, (ROWS, 128), 0)
    in_row = lax.broadcasted_iota(jnp.int32, (ROWS, 128), 1)
    pick = (in_row == (out_row // 12) * 16 + out_row % 12).astype(jnp.bfloat16)
    w_own[...] = jnp.dot(
        pick, w_recv[...].reshape(128, F), preferred_element_type=jnp.float32
    ).astype(jnp.bfloat16)

    def slot(b, plane):
        held = y_lo if b == 0 else 1 - y_lo
        first = pl.multiple_of(dp_of(held, plane, core) * ROWS, ROWS)
        return w_all.at[pl.ds(first, ROWS)]

    pending = []

    def ring(way, step, b, src, plane):
        copy = remote(
            src, slot(b, plane), z_send.at[way, step, b], z_recv.at[way, step, b],
            up if way == 0 else down,
        )
        copy.start()
        pending.append(copy)

    def landed(way, step, b):
        plane = (z + (8 - step if way == 0 else step)) % 8
        ref = slot(b, plane)
        remote(
            ref, ref, z_send.at[way, step - 1, b], z_recv.at[way, step - 1, b],
            up if way == 0 else down,
        ).wait_recv()
        return ref, plane

    across = []

    def to_sibling(src, dst):
        n = len(across)
        copy = remote(src, dst, s_send.at[n], s_recv.at[n], sibling)
        copy.start()
        across.append(copy)

    taken = [0]

    def from_sibling(upto):
        for n in range(taken[0], upto):
            across[n].wait_recv()
        taken[0] = upto

    own_slot = slot(0, z)
    to_partner = remote(w_own, own_slot, y_send.at[0], y_recv.at[0], partner)
    to_partner.start()
    ring(0, 0, 0, w_own, z)
    ring(1, 0, 0, w_own, z)
    to_sibling(w_own, own_slot)
    keep = pltpu.make_async_copy(w_own, own_slot, w_self.at[1])
    keep.start()

    def send_merged(j, a, rs):
        for r in rs:
            exchange(r, j, a).start()

    same_row = (1, 3, 5)
    other_row = (0, 2, 4, 6)
    for j in range(2):
        for a in range(2):
            send_merged(j, a, same_row)
    selfs = []
    for j in range(2):
        copy = pltpu.make_async_copy(send.at[me, j], recv.at[j, me], self_sem.at[j])
        copy.start()
        selfs.append(copy)

    def from_partner():
        other = slot(1, z)
        remote(other, other, y_send.at[0], y_recv.at[0], partner).wait_recv()
        ring(0, 0, 1, other, z)
        ring(1, 0, 1, other, z)
        to_sibling(other, other)

    def ring_step(step, b, ways=(0, 1)):
        for way in ways:
            if step == 4 and way != b:
                continue
            ref, plane = landed(way, step, b)
            if step < 3 or (step == 3 and way == b):
                ring(way, step, b, ref, plane)
            to_sibling(ref, ref)

    gap = gap_ref[0, 0]

    def attend(j):
        for a in range(2):
            for r in range(7):
                exchange(r, j, a).wait_recv()
        selfs[j].wait()
        for t in range(8):
            here = pl.ds(t * TOK, TOK)
            k2[here, :HD] = recv[j, t, 1]
            k2[here, HD:] = recv[j, t, 3]
            v2[here, :HD] = recv[j, t, 4]
            v2[here, HD:] = recv[j, t, 5]

        def block(n, carry):
            q = recv[j, pl.ds(2 * n, 2), 0].reshape(2 * TOK, HD)
            tq = recv[j, pl.ds(2 * n, 2), 2].reshape(2 * TOK, HD)
            scores = dot_t(q, k2[:, :HD])
            scores_dot = dot_t(jnp.concatenate([tq, q], axis=1), k2[...])
            highest = jnp.max(scores, axis=1, keepdims=True)
            weights = jnp.exp((scores - highest) * SCALE)
            total = jnp.sum(weights, axis=1, keepdims=True)
            mean = jnp.sum(weights * scores_dot, axis=1, keepdims=True) / total
            tangent = (weights * (scores_dot - mean)).astype(jnp.bfloat16)
            mixed = jnp.dot(
                weights.astype(jnp.bfloat16), v2[...], preferred_element_type=jnp.float32
            )
            moved = jnp.dot(tangent, v2[:, :HD], preferred_element_type=jnp.float32)
            norm = 1.0 / total
            attn = mixed[:, :HD] * norm
            attn_dot = (moved * SCALE + mixed[:, HD:]) * norm
            both = (attn + gap * attn_dot).astype(jnp.bfloat16)
            start = pl.multiple_of(n * 2 * TOK, 2 * TOK)
            own[j, pl.ds(start, 2 * TOK)] = attn.astype(jnp.bfloat16)
            send2[j, pl.ds(2 * n, 2)] = both.reshape(2, TOK, HD)
            return carry

        lax.fori_loop(0, 4, block, 0)

    def back(r, j):
        col = pl.multiple_of(me * GROUP + j * HD, HD)
        return remote(
            send2.at[j, peers[r]], tok.at[:, pl.ds(col, HD)], p_send.at[r, j], p_recv.at[r, j],
            (dp, peers[r]),
        )

    def along(dx, j):
        col = pl.multiple_of(x * GROUP + j * HD, HD)
        return remote(
            own.at[j], full.at[:, pl.ds(col, HD)], f_send.at[dx - 1, j], f_recv.at[dx - 1, j],
            (dp, y_hi * 4 + (x + dx) % 4),
        )

    locals_ = []

    def hand_out(j):
        for r in range(7):
            back(r, j).start()
        col = pl.multiple_of(me * GROUP + j * HD, HD)
        copy = pltpu.make_async_copy(send2.at[j, me], tok.at[:, pl.ds(col, HD)], self_sem.at[2 + j])
        copy.start()
        locals_.append(copy)
        col = pl.multiple_of(x * GROUP + j * HD, HD)
        copy = pltpu.make_async_copy(own.at[j], full.at[:, pl.ds(col, HD)], self_sem.at[4 + j])
        copy.start()
        locals_.append(copy)

    def hand_along(j):
        for dx in (1, 3, 2):
            along(dx, j).start()

    from_partner()
    send_merged(0, 0, other_row)
    send_merged(0, 1, other_row)
    ring_step(1, 0)
    send_merged(1, 0, other_row)
    ring_step(2, 0)
    send_merged(1, 1, other_row)
    attend(0)
    hand_out(0)
    hand_along(0)
    ring_step(1, 1)
    ring_step(3, 0)
    attend(1)
    hand_out(1)
    ring_step(2, 1)
    vel_load.wait()
    for j in range(2):
        for r in range(7):
            back(r, j).wait_recv()
    hand_along(1)
    for copy in locals_:
        copy.wait()
    keep.wait()

    near = z // 2
    side = 1 - 2 * (z % 2)
    pairs = (near, (near + 4 - side) % 4, (near + side) % 4, (near + 2) % 4)

    def quarter_copy(n, lo, way):
        pair = pairs[n]
        to = 2 * lo + pair // 2
        half = pair % 2
        col = pl.multiple_of(me * TOK, TOK)
        y_to = (y_hi + way) % 2
        return remote(
            c_send_buf.at[n, lo], quarter.at[half, :, pl.ds(col, TOK)],
            c_send.at[n, lo, way], c_recv.at[half, way * 4 + (to + 4 - x) % 4],
            (dp, y_to * 4 + to),
        )

    def local_quarter(n, lo):
        half = pairs[n] % 2
        col = pl.multiple_of(me * TOK, TOK)
        return pltpu.make_async_copy(
            c_send_buf.at[n, lo], quarter.at[half, :, pl.ds(col, TOK)], self_sem.at[6 + half]
        )

    def project(n):
        pair = pairs[n]
        for lo in range(2):
            first = pl.multiple_of(lo * 1536 + pair * 384, 384)
            weights = w_all[pl.ds(first, 384)]
            proj = dot_t(tok[...], weights)
            moved = jnp.dot(
                onehot, vel[:, pl.ds(first, 384)], preferred_element_type=jnp.float32
            )
            cot = counts * proj - moved
            c_send_buf[n, lo] = cot.T.astype(jnp.bfloat16)
            to = 2 * lo + pair // 2
            quarter_copy(n, lo, 1).start()

            @pl.when(to != x)
            def _():
                quarter_copy(n, lo, 0).start()

            @pl.when(to == x)
            def _():
                local_quarter(n, lo).start()

            part = jnp.dot(cot.astype(jnp.bfloat16), weights, preferred_element_type=jnp.float32)
            if n == 0 and lo == 0:
                acc[...] = part
            else:
                acc[...] += part

    early = (near % 2 + (near // 2 + x) % 2) % 2
    halves = (early, 1 - early)

    from_sibling(8)
    project(0)
    ring_step(4, 0)
    ring_step(3, 1, (1,))
    from_sibling(12)
    project(1)
    ring_step(3, 1, (0,))
    from_sibling(15)
    project(2)
    ring_step(4, 1)
    from_sibling(16)
    project(3)

    def grads(r):
        here = pl.ds(pl.multiple_of(me * TOK, TOK), TOK)
        return remote(
            g_buf.at[peers[r]], ga_ref.at[here], g_send.at[r], g_recv.at[r], (dp, peers[r])
        )

    for h in range(8):
        g_buf[h] = acc[:, h * GROUP : (h + 1) * GROUP].astype(jnp.bfloat16)
    for r in range(7):
        grads(r).start()
    ga_own = pltpu.make_async_copy(
        g_buf.at[me], ga_ref.at[pl.ds(pl.multiple_of(me * TOK, TOK), TOK)], self_sem.at[8]
    )
    ga_own.start()

    def half_term(half):
        for way in range(2):
            for dx in range(4):
                if way or dx:
                    col = pl.multiple_of(me * TOK, TOK)
                    remote(
                        c_send_buf.at[0, 0], quarter.at[half, :, pl.ds(col, TOK)],
                        c_send.at[0, 0, 0], c_recv.at[half, way * 4 + dx], sibling,
                    ).wait_recv()
        pltpu.make_async_copy(
            c_send_buf.at[0, 0], quarter.at[half, :, pl.ds(0, TOK)], self_sem.at[6 + half]
        ).wait()
        for block in range(4):
            part = jnp.dot(
                quarter[half], full[:, block * GROUP : (block + 1) * GROUP],
                preferred_element_type=jnp.float32,
            )
            for zi in range(2):
                for c in range(2):
                    top = zi * 192 + c * ROWS
                    term[half, c, zi, block] = part[top : top + ROWS]
        copy = swap(half)
        copy.start()

    def swap(half):
        return remote(
            term.at[half, 1 - core], term_sib.at[half], b_send.at[half], b_recv.at[half], sibling
        )

    def reduce_copy(half, dz):
        turn_to = (z + dz + 7) % 8
        zi = turn_to // 4
        block = turn_to % 4
        lo = (half + block + 1) % 2
        rel = ((lo + y_lo) % 2) * 8 + dz
        return lo, zi, block, remote(
            rs_buf.at[half, zi, block], rs_recv.at[rel], r_send.at[half, dz], r_recv.at[rel],
            (dp_of(lo, (z + dz) % 8, core), me),
        )

    def spread(half):
        swap(half).wait_recv()
        for dz in (4, 3, 5, 2, 6, 1, 7, 0):
            lo, zi, block, copy = reduce_copy(half, dz)
            rs_buf[half, zi, block] = (
                term[half, core, zi, block] + term_sib[half, zi, block]
            ).astype(jnp.bfloat16)
            if dz:
                copy.start()
            else:

                @pl.when(lo != y_lo)
                def _():
                    copy.start()

                @pl.when(lo == y_lo)
                def _():
                    rs_recv[0] = rs_buf[half, zi, block]

    for dx in (1, 3, 2):
        for j in range(2):
            along(dx, j).wait_recv()
    half_term(halves[0])
    spread(halves[0])
    half_term(halves[1])
    spread(halves[1])

    for rel in range(1, 16):
        remote(
            rs_buf.at[0, 0, 0], rs_recv.at[rel], r_send.at[0, 0], r_recv.at[rel], sibling
        ).wait_recv()

    def add(rel, total):
        return total + rs_recv[rel].astype(jnp.float32)

    fin[...] = lax.fori_loop(0, 16, add, jnp.zeros((ROWS, GROUP), jnp.float32))
    place_copy = remote(fin, gw_ref, e_send.at[0], e_recv.at[0], dest)
    place_copy.start()

    to_partner.wait_send()
    for copy in pending:
        copy.wait_send()
    for copy in across:
        copy.wait_send()
    for r in range(7):
        for j in range(2):
            back(r, j).wait_send()
            for a in range(2):
                exchange(r, j, a).wait_send()
        grads(r).wait()
    ga_own.wait()
    for dx in (1, 3, 2):
        for j in range(2):
            along(dx, j).wait_send()
    for n in range(4):
        for lo in range(2):
            quarter_copy(n, lo, 1).wait_send()

            @pl.when(2 * lo + pairs[n] // 2 != x)
            def _():
                quarter_copy(n, lo, 0).wait_send()

    for half in range(2):
        swap(half).wait_send()
        for dz in range(8):
            lo, _, _, copy = reduce_copy(half, dz)
            if dz:
                copy.wait_send()
            else:

                @pl.when(lo != y_lo)
                def _():
                    copy.wait_send()

    place_copy.wait()


def clip_call(queries, key_states, queries_dot, keys_dot, value_states, values_dot, velocity, slot, gap, w_in):
    any_spec = pl.BlockSpec(memory_space=pl.ANY)
    vmem = pl.BlockSpec(memory_space=pltpu.VMEM)
    bf = jnp.bfloat16
    f32 = jnp.float32
    dma = pltpu.SemaphoreType.DMA
    return pl.pallas_call(
        clip_kernel,
        out_shape=(
            jax.ShapeDtypeStruct((MERGED, GROUP), bf),
            jax.ShapeDtypeStruct((ROWS, GROUP), f32),
        ),
        in_specs=[any_spec] * 7 + [vmem, pl.BlockSpec(memory_space=pltpu.SMEM), vmem],
        out_specs=(vmem, vmem),
        scratch_shapes=[
            pltpu.VMEM((16, F), bf),
            pltpu.VMEM((6, SRC_DEV, F), bf),
            pltpu.VMEM((SRC_DEV, D), bf),
            pltpu.VMEM((8, 2, 6, TOK, HD), bf),
            pltpu.VMEM((2, 8, 6, TOK, HD), bf),
            pltpu.VMEM((2, 8, TOK, HD), bf),
            pltpu.VMEM((2, MERGED, HD), bf),
            pltpu.VMEM((MERGED, 2 * HD), bf),
            pltpu.VMEM((MERGED, 2 * HD), bf),
            pltpu.VMEM((8, 16, F), bf),
            pltpu.VMEM((ROWS, F), bf),
            pltpu.VMEM((D, F), bf),
            pltpu.VMEM((TOK, F), bf),
            pltpu.VMEM((MERGED, 4 * GROUP), bf),
            pltpu.VMEM((TOK, F), f32),
            pltpu.VMEM((4, 2, 384, TOK), bf),
            pltpu.VMEM((2, 384, MERGED), bf),
            pltpu.VMEM((8, TOK, GROUP), bf),
            pltpu.VMEM((2, 2, 2, 4, ROWS, GROUP), f32),
            pltpu.VMEM((2, 2, 4, ROWS, GROUP), f32),
            pltpu.VMEM((2, 2, 4, ROWS, GROUP), bf),
            pltpu.VMEM((16, ROWS, GROUP), bf),
            pltpu.VMEM((ROWS, GROUP), f32),
            dma((7,)),
            dma((9,)),
            dma((7, 2, 2)),
            dma((7, 2, 2)),
            dma((7, 2)),
            dma((7, 2)),
            dma((3, 2)),
            dma((3, 2)),
            dma((7,)),
            dma((7,)),
            dma((2,)),
            dma((1,)),
            dma((1,)),
            dma((2, 4, 2)),
            dma((2, 4, 2)),
            dma((16,)),
            dma((16,)),
            dma((4, 2, 2)),
            dma((2, 8)),
            dma((7,)),
            dma((7,)),
            dma((2,)),
            dma((2,)),
            dma((2, 8)),
            dma((16,)),
            dma((1,)),
            dma((1,)),
        ],
        compiler_params=pltpu.CompilerParams(
            collective_id=0, has_side_effects=True, vmem_limit_bytes=60 << 20
        ),
        cost_estimate=pl.CostEstimate(
            flops=10_000_000_000, bytes_accessed=9 << 20, transcendentals=2 << 20
        ),
    )(
        queries, key_states, queries_dot, keys_dot, value_states, values_dot, velocity,
        slot, gap, w_in,
    )


def on_device(
    queries, key_states, value_states, queries_dot, keys_dot, values_dot,
    velocity, time_gap, merge_slot, out_weight,
):
    grad_attn, grad_weight = clip_call(
        queries[0], key_states[0], queries_dot[0], keys_dot[0], value_states[0], values_dot[0],
        velocity[0], merge_slot, time_gap.reshape(1, 1), out_weight,
    )
    return (grad_attn[None], grad_weight)


def solution(mesh):
    block = P("dp", "head", None)
    return jax.shard_map(
        on_device,
        mesh=mesh,
        in_specs=(block,) * 7 + (P("dp"), P("dp", "head"), P(("dp", "head"), None)),
        out_specs=(P("dp", None, "head"), P("dp", "head")),
        check_vma=False,
    )
```

```python
import math

import jax
import jax.numpy as jnp
from jax import lax
from jax.experimental import pallas as pl
from jax.experimental.pallas import tpu as pltpu
from jax.sharding import PartitionSpec as P

MESH = pl.DeviceIdType.MESH
HD = 128
GROUP = 256
TOK = 128
SRC_DEV = 256
MERGED = 1024
F = 2048
D = 3072
ROWS = 96
SCALE = 1.0 / math.sqrt(HD)

PEERS = ((0, 1), (1, 0), (1, 1), (3, 0), (3, 1), (2, 0), (2, 1))


def place():
    dp = lax.axis_index("dp")
    head = lax.axis_index("head")
    return dp // 16, (dp // 2) % 8, dp % 2, head // 4, head % 4


def dp_of(y_lo, z, core):
    return y_lo * 16 + z * 2 + core


def dot_t(a, b):
    return lax.dot_general(a, b, (((1,), (1,)), ((), ())), preferred_element_type=jnp.float32)


def clip_kernel(
    q_hbm, k_hbm, tq_hbm, tk_hbm, v_hbm, tv_hbm, vel_hbm, slot_ref, gap_ref, w_in,
    ga_ref, gw_ref,
    w_pad, stage, vel, send, recv, send2, own, k2, v2, w_recv, w_own, w_all, tok, full, acc,
    c_send_buf, quarter, g_buf, term, term_sib, rs_buf, rs_recv, fin,
    in_sem, self_sem, a_send, a_recv, p_send, p_recv, f_send, f_recv, w_send, w_rcv, w_self,
    y_send, y_recv, z_send, z_recv, s_send, s_recv, c_send, c_recv, g_send, g_recv,
    b_send, b_recv, r_send, r_recv, e_send, e_recv,
):
    y_lo, z, core, y_hi, x = place()
    dp = lax.axis_index("dp")
    me = y_hi * 4 + x

    peers = [((y_hi + dy) % 2) * 4 + (x + dx) % 4 for dx, dy in PEERS]
    sibling = (dp_of(y_lo, z, 1 - core), me)
    partner = (dp_of(1 - y_lo, z, core), me)
    up = (dp_of(y_lo, (z + 1) % 8, core), me)
    down = (dp_of(y_lo, (z + 7) % 8, core), me)

    turn = (z + 7) % 8
    dest_x = turn % 4
    dest_z = 4 * (x % 2) + 2 * ((y_lo + dest_x + 1) % 2) + turn // 4
    dest = (dp_of(x // 2, dest_z, core), y_hi * 4 + dest_x)
    from_x = 2 * y_lo + z // 4
    from_z = (((z % 4) % 2) * 4 + x + 1) % 8
    source = (dp_of(((z % 4) // 2 + x + 1) % 2, from_z, core), y_hi * 4 + from_x)

    barrier = pltpu.get_barrier_semaphore()

    def greet(who):
        pl.semaphore_signal(barrier, inc=1, device_id=who, device_id_type=MESH)

    for p in peers:
        greet((dp, p))
    for dy in range(2):
        for dz in range(8):
            if dy or dz:
                greet((dp_of((y_lo + dy) % 2, (z + dz) % 8, core), me))
    greet(sibling)
    greet(dest)
    greet(source)

    loads = []
    for i, ref in enumerate((q_hbm, k_hbm, tq_hbm, tk_hbm, v_hbm, tv_hbm)):
        load = pltpu.make_async_copy(ref, stage.at[i], in_sem.at[i])
        load.start()
        loads.append(load)
    vel_load = pltpu.make_async_copy(vel_hbm, vel, in_sem.at[6])
    vel_load.start()
    w_pad[...] = jnp.zeros_like(w_pad)
    w_pad[:12] = w_in[...]

    def remote(src, dst, ssem, rsem, who):
        return pltpu.make_async_remote_copy(
            src_ref=src, dst_ref=dst, send_sem=ssem, recv_sem=rsem,
            device_id=who, device_id_type=MESH,
        )

    rows = lax.broadcasted_iota(jnp.int32, (TOK, SRC_DEV), 0)
    select = slot_ref[...] == rows
    counts = jnp.sum(select.astype(jnp.float32), axis=1, keepdims=True)
    inverse = 1.0 / counts
    onehot = select.astype(jnp.bfloat16)

    def merge(i):
        loads[i].wait()

        def body(n, carry):
            col = pl.multiple_of(n * 4 * GROUP, 4 * GROUP)
            total = jnp.dot(
                onehot, stage[i, :, pl.ds(col, 4 * GROUP)], preferred_element_type=jnp.float32
            )
            merged = (total * inverse).astype(jnp.bfloat16)
            for h in range(4):
                for j in range(2):
                    first = h * GROUP + j * HD
                    send[4 * n + h, j, i] = merged[:, first : first + HD]
            return carry

        lax.fori_loop(0, 2, body, 0)

    def exchange(r, j, a):
        return remote(
            send.at[peers[r], j, pl.ds(3 * a, 3)],
            recv.at[j, me, pl.ds(3 * a, 3)],
            a_send.at[r, j, a],
            a_recv.at[r, j, a],
            (dp, peers[r]),
        )

    for i in range(6):
        merge(i)
    pl.semaphore_wait(barrier, 25)

    w_copies = []
    for r in range(7):
        copy = remote(w_pad, w_recv.at[me], w_send.at[r], w_rcv.at[r], (dp, peers[r]))
        copy.start()
        w_copies.append(copy)
    w_local = pltpu.make_async_copy(w_pad, w_recv.at[me], w_self.at[0])
    w_local.start()

    for copy in w_copies:
        copy.wait()
    w_local.wait()
    out_row = lax.broadcasted_iota(jnp.int32, (ROWS, 128), 0)
    in_row = lax.broadcasted_iota(jnp.int32, (ROWS, 128), 1)
    pick = (in_row == (out_row // 12) * 16 + out_row % 12).astype(jnp.bfloat16)
    w_own[...] = jnp.dot(
        pick, w_recv[...].reshape(128, F), preferred_element_type=jnp.float32
    ).astype(jnp.bfloat16)

    def slot(b, plane):
        held = y_lo if b == 0 else 1 - y_lo
        first = pl.multiple_of(dp_of(held, plane, core) * ROWS, ROWS)
        return w_all.at[pl.ds(first, ROWS)]

    pending = []

    def ring(way, step, b, src, plane):
        copy = remote(
            src, slot(b, plane), z_send.at[way, step, b], z_recv.at[way, step, b],
            up if way == 0 else down,
        )
        copy.start()
        pending.append(copy)

    def landed(way, step, b):
        plane = (z + (8 - step if way == 0 else step)) % 8
        ref = slot(b, plane)
        remote(
            ref, ref, z_send.at[way, step - 1, b], z_recv.at[way, step - 1, b],
            up if way == 0 else down,
        ).wait_recv()
        return ref, plane

    across = []

    def to_sibling(src, dst):
        n = len(across)
        copy = remote(src, dst, s_send.at[n], s_recv.at[n], sibling)
        copy.start()
        across.append(copy)

    taken = [0]

    def from_sibling(upto):
        for n in range(taken[0], upto):
            across[n].wait_recv()
        taken[0] = upto

    own_slot = slot(0, z)
    to_partner = remote(w_own, own_slot, y_send.at[0], y_recv.at[0], partner)
    to_partner.start()
    ring(0, 0, 0, w_own, z)
    ring(1, 0, 0, w_own, z)
    to_sibling(w_own, own_slot)
    keep = pltpu.make_async_copy(w_own, own_slot, w_self.at[1])
    keep.start()

    def send_merged(j, a, rs):
        for r in rs:
            exchange(r, j, a).start()

    same_row = (1, 3, 5)
    other_row = (0, 2, 4, 6)
    for j in range(2):
        for a in range(2):
            send_merged(j, a, same_row)
    selfs = []
    for j in range(2):
        copy = pltpu.make_async_copy(send.at[me, j], recv.at[j, me], self_sem.at[j])
        copy.start()
        selfs.append(copy)

    def from_partner():
        other = slot(1, z)
        remote(other, other, y_send.at[0], y_recv.at[0], partner).wait_recv()
        ring(0, 0, 1, other, z)
        ring(1, 0, 1, other, z)
        to_sibling(other, other)

    def ring_step(step, b, ways=(0, 1)):
        for way in ways:
            if step == 4 and way != b:
                continue
            ref, plane = landed(way, step, b)
            if step < 3 or (step == 3 and way == b):
                ring(way, step, b, ref, plane)
            to_sibling(ref, ref)

    gap = gap_ref[0, 0]

    def attend(j):
        for a in range(2):
            for r in range(7):
                exchange(r, j, a).wait_recv()
        selfs[j].wait()
        for t in range(8):
            here = pl.ds(t * TOK, TOK)
            k2[here, :HD] = recv[j, t, 1]
            k2[here, HD:] = recv[j, t, 3]
            v2[here, :HD] = recv[j, t, 4]
            v2[here, HD:] = recv[j, t, 5]

        def block(n, carry):
            q = recv[j, pl.ds(2 * n, 2), 0].reshape(2 * TOK, HD)
            tq = recv[j, pl.ds(2 * n, 2), 2].reshape(2 * TOK, HD)
            scores = dot_t(q, k2[:, :HD])
            scores_dot = dot_t(jnp.concatenate([tq, q], axis=1), k2[...])
            highest = jnp.max(scores, axis=1, keepdims=True)
            weights = jnp.exp((scores - highest) * SCALE)
            total = jnp.sum(weights, axis=1, keepdims=True)
            mean = jnp.sum(weights * scores_dot, axis=1, keepdims=True) / total
            tangent = (weights * (scores_dot - mean)).astype(jnp.bfloat16)
            mixed = jnp.dot(
                weights.astype(jnp.bfloat16), v2[...], preferred_element_type=jnp.float32
            )
            moved = jnp.dot(tangent, v2[:, :HD], preferred_element_type=jnp.float32)
            norm = 1.0 / total
            attn = mixed[:, :HD] * norm
            attn_dot = (moved * SCALE + mixed[:, HD:]) * norm
            both = (attn + gap * attn_dot).astype(jnp.bfloat16)
            start = pl.multiple_of(n * 2 * TOK, 2 * TOK)
            own[j, pl.ds(start, 2 * TOK)] = attn.astype(jnp.bfloat16)
            send2[j, pl.ds(2 * n, 2)] = both.reshape(2, TOK, HD)
            return carry

        lax.fori_loop(0, 4, block, 0)

    def back(r, j):
        col = pl.multiple_of(me * GROUP + j * HD, HD)
        return remote(
            send2.at[j, peers[r]], tok.at[:, pl.ds(col, HD)], p_send.at[r, j], p_recv.at[r, j],
            (dp, peers[r]),
        )

    def along(dx, j):
        col = pl.multiple_of(x * GROUP + j * HD, HD)
        return remote(
            own.at[j], full.at[:, pl.ds(col, HD)], f_send.at[dx - 1, j], f_recv.at[dx - 1, j],
            (dp, y_hi * 4 + (x + dx) % 4),
        )

    locals_ = []

    def hand_out(j):
        for r in range(7):
            back(r, j).start()
        col = pl.multiple_of(me * GROUP + j * HD, HD)
        copy = pltpu.make_async_copy(send2.at[j, me], tok.at[:, pl.ds(col, HD)], self_sem.at[2 + j])
        copy.start()
        locals_.append(copy)
        col = pl.multiple_of(x * GROUP + j * HD, HD)
        copy = pltpu.make_async_copy(own.at[j], full.at[:, pl.ds(col, HD)], self_sem.at[4 + j])
        copy.start()
        locals_.append(copy)

    def hand_along(j):
        for dx in (1, 3, 2):
            along(dx, j).start()

    from_partner()
    send_merged(0, 0, other_row)
    send_merged(0, 1, other_row)
    ring_step(1, 0)
    send_merged(1, 0, other_row)
    ring_step(2, 0)
    send_merged(1, 1, other_row)
    attend(0)
    hand_out(0)
    hand_along(0)
    ring_step(1, 1)
    ring_step(3, 0)
    attend(1)
    hand_out(1)
    ring_step(2, 1)
    vel_load.wait()
    for j in range(2):
        for r in range(7):
            back(r, j).wait_recv()
    hand_along(1)
    for copy in locals_:
        copy.wait()
    keep.wait()

    near = z // 2
    side = 1 - 2 * (z % 2)
    pairs = (near, (near + 4 - side) % 4, (near + side) % 4, (near + 2) % 4)

    def quarter_copy(n, lo, way):
        pair = pairs[n]
        to = 2 * lo + pair // 2
        half = pair % 2
        col = pl.multiple_of(me * TOK, TOK)
        y_to = (y_hi + way) % 2
        return remote(
            c_send_buf.at[n, lo], quarter.at[half, :, pl.ds(col, TOK)],
            c_send.at[n, lo, way], c_recv.at[half, way * 4 + (to + 4 - x) % 4],
            (dp, y_to * 4 + to),
        )

    def local_quarter(n, lo):
        half = pairs[n] % 2
        col = pl.multiple_of(me * TOK, TOK)
        return pltpu.make_async_copy(
            c_send_buf.at[n, lo], quarter.at[half, :, pl.ds(col, TOK)], self_sem.at[6 + half]
        )

    def project(n):
        pair = pairs[n]
        for lo in range(2):
            first = pl.multiple_of(lo * 1536 + pair * 384, 384)
            weights = w_all[pl.ds(first, 384)]
            proj = dot_t(tok[...], weights)
            moved = jnp.dot(
                onehot, vel[:, pl.ds(first, 384)], preferred_element_type=jnp.float32
            )
            cot = counts * proj - moved
            c_send_buf[n, lo] = cot.T.astype(jnp.bfloat16)
            to = 2 * lo + pair // 2
            quarter_copy(n, lo, 1).start()

            @pl.when(to != x)
            def _():
                quarter_copy(n, lo, 0).start()

            @pl.when(to == x)
            def _():
                local_quarter(n, lo).start()

            part = jnp.dot(cot.astype(jnp.bfloat16), weights, preferred_element_type=jnp.float32)
            if n == 0 and lo == 0:
                acc[...] = part
            else:
                acc[...] += part

    early = (near % 2 + (near // 2 + x) % 2) % 2
    halves = (early, 1 - early)

    from_sibling(8)
    project(0)
    ring_step(4, 0)
    ring_step(3, 1, (1,))
    from_sibling(12)
    project(1)
    ring_step(3, 1, (0,))
    from_sibling(15)
    project(2)
    ring_step(4, 1)
    from_sibling(16)
    project(3)

    def grads(r):
        here = pl.ds(pl.multiple_of(me * TOK, TOK), TOK)
        return remote(
            g_buf.at[peers[r]], ga_ref.at[here], g_send.at[r], g_recv.at[r], (dp, peers[r])
        )

    for h in range(8):
        g_buf[h] = acc[:, h * GROUP : (h + 1) * GROUP].astype(jnp.bfloat16)
    for r in range(7):
        grads(r).start()
    ga_own = pltpu.make_async_copy(
        g_buf.at[me], ga_ref.at[pl.ds(pl.multiple_of(me * TOK, TOK), TOK)], self_sem.at[8]
    )
    ga_own.start()

    def half_term(half):
        for way in range(2):
            for dx in range(4):
                if way or dx:
                    col = pl.multiple_of(me * TOK, TOK)
                    remote(
                        c_send_buf.at[0, 0], quarter.at[half, :, pl.ds(col, TOK)],
                        c_send.at[0, 0, 0], c_recv.at[half, way * 4 + dx], sibling,
                    ).wait_recv()
        pltpu.make_async_copy(
            c_send_buf.at[0, 0], quarter.at[half, :, pl.ds(0, TOK)], self_sem.at[6 + half]
        ).wait()
        for block in range(4):
            part = jnp.dot(
                quarter[half], full[:, block * GROUP : (block + 1) * GROUP],
                preferred_element_type=jnp.float32,
            )
            for zi in range(2):
                for c in range(2):
                    top = zi * 192 + c * ROWS
                    term[half, c, zi, block] = part[top : top + ROWS]
        copy = swap(half)
        copy.start()

    def swap(half):
        return remote(
            term.at[half, 1 - core], term_sib.at[half], b_send.at[half], b_recv.at[half], sibling
        )

    def reduce_copy(half, dz):
        turn_to = (z + dz + 7) % 8
        zi = turn_to // 4
        block = turn_to % 4
        lo = (half + block + 1) % 2
        rel = ((lo + y_lo) % 2) * 8 + dz
        return lo, zi, block, remote(
            rs_buf.at[half, zi, block], rs_recv.at[rel], r_send.at[half, dz], r_recv.at[rel],
            (dp_of(lo, (z + dz) % 8, core), me),
        )

    def spread(half):
        swap(half).wait_recv()
        for dz in (4, 3, 5, 2, 6, 1, 7, 0):
            lo, zi, block, copy = reduce_copy(half, dz)
            rs_buf[half, zi, block] = (
                term[half, core, zi, block] + term_sib[half, zi, block]
            ).astype(jnp.bfloat16)
            if dz:
                copy.start()
            else:

                @pl.when(lo != y_lo)
                def _():
                    copy.start()

                @pl.when(lo == y_lo)
                def _():
                    rs_recv[0] = rs_buf[half, zi, block]

    for dx in (1, 3, 2):
        for j in range(2):
            along(dx, j).wait_recv()
    half_term(halves[0])
    spread(halves[0])
    half_term(halves[1])
    spread(halves[1])

    for rel in range(1, 16):
        remote(
            rs_buf.at[0, 0, 0], rs_recv.at[rel], r_send.at[0, 0], r_recv.at[rel], sibling
        ).wait_recv()

    def add(rel, total):
        return total + rs_recv[rel].astype(jnp.float32)

    fin[...] = lax.fori_loop(0, 16, add, jnp.zeros((ROWS, GROUP), jnp.float32))
    place_copy = remote(fin, gw_ref, e_send.at[0], e_recv.at[0], dest)
    place_copy.start()

    to_partner.wait_send()
    for copy in pending:
        copy.wait_send()
    for copy in across:
        copy.wait_send()
    for r in range(7):
        for j in range(2):
            back(r, j).wait_send()
            for a in range(2):
                exchange(r, j, a).wait_send()
        grads(r).wait()
    ga_own.wait()
    for dx in (1, 3, 2):
        for j in range(2):
            along(dx, j).wait_send()
    for n in range(4):
        for lo in range(2):
            quarter_copy(n, lo, 1).wait_send()

            @pl.when(2 * lo + pairs[n] // 2 != x)
            def _():
                quarter_copy(n, lo, 0).wait_send()

    for half in range(2):
        swap(half).wait_send()
        for dz in range(8):
            lo, _, _, copy = reduce_copy(half, dz)
            if dz:
                copy.wait_send()
            else:

                @pl.when(lo != y_lo)
                def _():
                    copy.wait_send()

    place_copy.wait()


def clip_call(queries, key_states, queries_dot, keys_dot, value_states, values_dot, velocity, slot, gap, w_in):
    any_spec = pl.BlockSpec(memory_space=pl.ANY)
    vmem = pl.BlockSpec(memory_space=pltpu.VMEM)
    bf = jnp.bfloat16
    f32 = jnp.float32
    dma = pltpu.SemaphoreType.DMA
    return pl.pallas_call(
        clip_kernel,
        out_shape=(
            jax.ShapeDtypeStruct((MERGED, GROUP), bf),
            jax.ShapeDtypeStruct((ROWS, GROUP), f32),
        ),
        in_specs=[any_spec] * 7 + [vmem, pl.BlockSpec(memory_space=pltpu.SMEM), vmem],
        out_specs=(any_spec, any_spec),
        scratch_shapes=[
            pltpu.VMEM((16, F), bf),
            pltpu.VMEM((6, SRC_DEV, F), bf),
            pltpu.VMEM((SRC_DEV, D), bf),
            pltpu.VMEM((8, 2, 6, TOK, HD), bf),
            pltpu.VMEM((2, 8, 6, TOK, HD), bf),
            pltpu.VMEM((2, 8, TOK, HD), bf),
            pltpu.VMEM((2, MERGED, HD), bf),
            pltpu.VMEM((MERGED, 2 * HD), bf),
            pltpu.VMEM((MERGED, 2 * HD), bf),
            pltpu.VMEM((8, 16, F), bf),
            pltpu.VMEM((ROWS, F), bf),
            pltpu.VMEM((D, F), bf),
            pltpu.VMEM((TOK, F), bf),
            pltpu.VMEM((MERGED, 4 * GROUP), bf),
            pltpu.VMEM((TOK, F), f32),
            pltpu.VMEM((4, 2, 384, TOK), bf),
            pltpu.VMEM((2, 384, MERGED), bf),
            pltpu.VMEM((8, TOK, GROUP), bf),
            pltpu.VMEM((2, 2, 2, 4, ROWS, GROUP), f32),
            pltpu.VMEM((2, 2, 4, ROWS, GROUP), f32),
            pltpu.VMEM((2, 2, 4, ROWS, GROUP), bf),
            pltpu.VMEM((16, ROWS, GROUP), bf),
            pltpu.VMEM((ROWS, GROUP), f32),
            dma((7,)),
            dma((9,)),
            dma((7, 2, 2)),
            dma((7, 2, 2)),
            dma((7, 2)),
            dma((7, 2)),
            dma((3, 2)),
            dma((3, 2)),
            dma((7,)),
            dma((7,)),
            dma((2,)),
            dma((1,)),
            dma((1,)),
            dma((2, 4, 2)),
            dma((2, 4, 2)),
            dma((16,)),
            dma((16,)),
            dma((4, 2, 2)),
            dma((2, 8)),
            dma((7,)),
            dma((7,)),
            dma((2,)),
            dma((2,)),
            dma((2, 8)),
            dma((16,)),
            dma((1,)),
            dma((1,)),
        ],
        compiler_params=pltpu.CompilerParams(
            collective_id=0, has_side_effects=True, vmem_limit_bytes=60 << 20
        ),
        cost_estimate=pl.CostEstimate(
            flops=10_000_000_000, bytes_accessed=9 << 20, transcendentals=2 << 20
        ),
    )(
        queries, key_states, queries_dot, keys_dot, value_states, values_dot, velocity,
        slot, gap, w_in,
    )


def on_device(
    queries, key_states, value_states, queries_dot, keys_dot, values_dot,
    velocity, time_gap, merge_slot, out_weight,
):
    grad_attn, grad_weight = clip_call(
        queries[0], key_states[0], queries_dot[0], keys_dot[0], value_states[0], values_dot[0],
        velocity[0], merge_slot, time_gap.reshape(1, 1), out_weight,
    )
    return (grad_attn[None], grad_weight)


def solution(mesh):
    block = P("dp", "head", None)
    return jax.shard_map(
        on_device,
        mesh=mesh,
        in_specs=(block,) * 7 + (P("dp"), P("dp", "head"), P(("dp", "head"), None)),
        out_specs=(P("dp", None, "head"), P("dp", "head")),
        check_vma=False,
    )
```

```python
import math

import jax
import jax.numpy as jnp
from jax import lax
from jax.experimental import pallas as pl
from jax.experimental.pallas import tpu as pltpu
from jax.sharding import PartitionSpec as P

MESH = pl.DeviceIdType.MESH
HD = 128
GROUP = 256
TOK = 128
SRC_DEV = 256
MERGED = 1024
F = 2048
D = 3072
ROWS = 96
SCALE = 1.0 / math.sqrt(HD)

PEERS = ((0, 1), (1, 0), (1, 1), (3, 0), (3, 1), (2, 0), (2, 1))


def place():
    dp = lax.axis_index("dp")
    head = lax.axis_index("head")
    return dp // 16, (dp // 2) % 8, dp % 2, head // 4, head % 4


def dp_of(y_lo, z, core):
    return y_lo * 16 + z * 2 + core


def dot_t(a, b):
    return lax.dot_general(a, b, (((1,), (1,)), ((), ())), preferred_element_type=jnp.float32)


def clip_kernel(
    q_hbm, k_hbm, tq_hbm, tk_hbm, v_hbm, tv_hbm, vel_hbm, slot_ref, gap_ref, w_in,
    ga_ref, gw_ref,
    w_pad, stage, vel, send, recv, send2, own, k2, v2, w_recv, w_own, w_all, tok, full, acc,
    c_send_buf, quarter, g_buf, term, term_out, term_sib, rs_buf, rs_recv, fin,
    in_sem, self_sem, a_send, a_recv, p_send, p_recv, f_send, f_recv, w_send, w_rcv, w_self,
    y_send, y_recv, z_send, z_recv, s_send, s_recv, c_send, c_recv, g_send, g_recv,
    b_send, b_recv, r_send, r_recv, e_send, e_recv,
):
    y_lo, z, core, y_hi, x = place()
    dp = lax.axis_index("dp")
    me = y_hi * 4 + x

    peers = [((y_hi + dy) % 2) * 4 + (x + dx) % 4 for dx, dy in PEERS]
    sibling = (dp_of(y_lo, z, 1 - core), me)
    partner = (dp_of(1 - y_lo, z, core), me)
    up = (dp_of(y_lo, (z + 1) % 8, core), me)
    down = (dp_of(y_lo, (z + 7) % 8, core), me)

    turn = (z + 7) % 8
    dest_x = turn % 4
    dest_z = 4 * (x % 2) + 2 * ((y_lo + dest_x + 1) % 2) + turn // 4
    dest = (dp_of(x // 2, dest_z, core), y_hi * 4 + dest_x)
    from_x = 2 * y_lo + z // 4
    from_z = (((z % 4) % 2) * 4 + x + 1) % 8
    source = (dp_of(((z % 4) // 2 + x + 1) % 2, from_z, core), y_hi * 4 + from_x)

    barrier = pltpu.get_barrier_semaphore()

    def greet(who):
        pl.semaphore_signal(barrier, inc=1, device_id=who, device_id_type=MESH)

    for p in peers:
        greet((dp, p))
    for dy in range(2):
        for dz in range(8):
            if dy or dz:
                greet((dp_of((y_lo + dy) % 2, (z + dz) % 8, core), me))
    greet(sibling)
    greet(dest)
    greet(source)

    loads = []
    for i, ref in enumerate((q_hbm, k_hbm, tq_hbm, tk_hbm, v_hbm, tv_hbm)):
        load = pltpu.make_async_copy(ref, stage.at[i], in_sem.at[i])
        load.start()
        loads.append(load)
    vel_load = pltpu.make_async_copy(vel_hbm, vel, in_sem.at[6])
    vel_load.start()
    w_pad[...] = jnp.zeros_like(w_pad)
    w_pad[:12] = w_in[...]

    def remote(src, dst, ssem, rsem, who):
        return pltpu.make_async_remote_copy(
            src_ref=src, dst_ref=dst, send_sem=ssem, recv_sem=rsem,
            device_id=who, device_id_type=MESH,
        )

    rows = lax.broadcasted_iota(jnp.int32, (TOK, SRC_DEV), 0)
    select = slot_ref[...] == rows
    counts = jnp.sum(select.astype(jnp.float32), axis=1, keepdims=True)
    inverse = 1.0 / counts
    onehot = select.astype(jnp.bfloat16)

    def merge(i):
        loads[i].wait()

        def body(n, carry):
            col = pl.multiple_of(n * 4 * GROUP, 4 * GROUP)
            total = jnp.dot(
                onehot, stage[i, :, pl.ds(col, 4 * GROUP)], preferred_element_type=jnp.float32
            )
            merged = (total * inverse).astype(jnp.bfloat16)
            for h in range(4):
                for j in range(2):
                    first = h * GROUP + j * HD
                    send[4 * n + h, j, i] = merged[:, first : first + HD]
            return carry

        lax.fori_loop(0, 2, body, 0)

    def exchange(r, j, a):
        return remote(
            send.at[peers[r], j, pl.ds(3 * a, 3)],
            recv.at[j, me, pl.ds(3 * a, 3)],
            a_send.at[r, j, a],
            a_recv.at[r, j, a],
            (dp, peers[r]),
        )

    for i in range(6):
        merge(i)
    pl.semaphore_wait(barrier, 25)

    w_copies = []
    for r in range(7):
        copy = remote(w_pad, w_recv.at[me], w_send.at[r], w_rcv.at[r], (dp, peers[r]))
        copy.start()
        w_copies.append(copy)
    w_local = pltpu.make_async_copy(w_pad, w_recv.at[me], w_self.at[0])
    w_local.start()

    for copy in w_copies:
        copy.wait()
    w_local.wait()
    out_row = lax.broadcasted_iota(jnp.int32, (ROWS, 128), 0)
    in_row = lax.broadcasted_iota(jnp.int32, (ROWS, 128), 1)
    pick = (in_row == (out_row // 12) * 16 + out_row % 12).astype(jnp.bfloat16)
    w_own[...] = jnp.dot(
        pick, w_recv[...].reshape(128, F), preferred_element_type=jnp.float32
    ).astype(jnp.bfloat16)

    def slot(b, plane):
        held = y_lo if b == 0 else 1 - y_lo
        first = pl.multiple_of(dp_of(held, plane, core) * ROWS, ROWS)
        return w_all.at[pl.ds(first, ROWS)]

    pending = []

    def ring(way, step, b, src, plane):
        copy = remote(
            src, slot(b, plane), z_send.at[way, step, b], z_recv.at[way, step, b],
            up if way == 0 else down,
        )
        copy.start()
        pending.append(copy)

    def landed(way, step, b):
        plane = (z + (8 - step if way == 0 else step)) % 8
        ref = slot(b, plane)
        remote(
            ref, ref, z_send.at[way, step - 1, b], z_recv.at[way, step - 1, b],
            up if way == 0 else down,
        ).wait_recv()
        return ref, plane

    across = []

    def to_sibling(src, dst):
        n = len(across)
        copy = remote(src, dst, s_send.at[n], s_recv.at[n], sibling)
        copy.start()
        across.append(copy)

    taken = [0]

    def from_sibling(upto):
        for n in range(taken[0], upto):
            across[n].wait_recv()
        taken[0] = upto

    own_slot = slot(0, z)
    to_partner = remote(w_own, own_slot, y_send.at[0], y_recv.at[0], partner)
    to_partner.start()
    ring(0, 0, 0, w_own, z)
    ring(1, 0, 0, w_own, z)
    to_sibling(w_own, own_slot)
    keep = pltpu.make_async_copy(w_own, own_slot, w_self.at[1])
    keep.start()

    def send_merged(j, a, rs):
        for r in rs:
            exchange(r, j, a).start()

    same_row = (1, 3, 5)
    other_row = (0, 2, 4, 6)
    for j in range(2):
        for a in range(2):
            send_merged(j, a, same_row)
    selfs = []
    for j in range(2):
        copy = pltpu.make_async_copy(send.at[me, j], recv.at[j, me], self_sem.at[j])
        copy.start()
        selfs.append(copy)

    def from_partner():
        other = slot(1, z)
        remote(other, other, y_send.at[0], y_recv.at[0], partner).wait_recv()
        ring(0, 0, 1, other, z)
        ring(1, 0, 1, other, z)
        to_sibling(other, other)

    def ring_step(step, b, ways=(0, 1)):
        for way in ways:
            if step == 4 and way != b:
                continue
            ref, plane = landed(way, step, b)
            if step < 3 or (step == 3 and way == b):
                ring(way, step, b, ref, plane)
            to_sibling(ref, ref)

    gap = gap_ref[0, 0]

    def attend(j):
        for a in range(2):
            for r in range(7):
                exchange(r, j, a).wait_recv()
        selfs[j].wait()
        for t in range(8):
            here = pl.ds(t * TOK, TOK)
            k2[here, :HD] = recv[j, t, 1]
            k2[here, HD:] = recv[j, t, 3]
            v2[here, :HD] = recv[j, t, 4]
            v2[here, HD:] = recv[j, t, 5]

        def block(n, carry):
            q = recv[j, pl.ds(2 * n, 2), 0].reshape(2 * TOK, HD)
            tq = recv[j, pl.ds(2 * n, 2), 2].reshape(2 * TOK, HD)
            scores = dot_t(q, k2[:, :HD])
            scores_dot = dot_t(jnp.concatenate([tq, q], axis=1), k2[...])
            highest = jnp.max(scores, axis=1, keepdims=True)
            weights = jnp.exp((scores - highest) * SCALE)
            total = jnp.sum(weights, axis=1, keepdims=True)
            mean = jnp.sum(weights * scores_dot, axis=1, keepdims=True) / total
            tangent = (weights * (scores_dot - mean)).astype(jnp.bfloat16)
            mixed = jnp.dot(
                weights.astype(jnp.bfloat16), v2[...], preferred_element_type=jnp.float32
            )
            moved = jnp.dot(tangent, v2[:, :HD], preferred_element_type=jnp.float32)
            norm = 1.0 / total
            attn = mixed[:, :HD] * norm
            attn_dot = (moved * SCALE + mixed[:, HD:]) * norm
            both = (attn + gap * attn_dot).astype(jnp.bfloat16)
            start = pl.multiple_of(n * 2 * TOK, 2 * TOK)
            own[j, pl.ds(start, 2 * TOK)] = attn.astype(jnp.bfloat16)
            send2[j, pl.ds(2 * n, 2)] = both.reshape(2, TOK, HD)
            return carry

        lax.fori_loop(0, 4, block, 0)

    def back(r, j):
        col = pl.multiple_of(me * GROUP + j * HD, HD)
        return remote(
            send2.at[j, peers[r]], tok.at[:, pl.ds(col, HD)], p_send.at[r, j], p_recv.at[r, j],
            (dp, peers[r]),
        )

    def along(dx, j):
        col = pl.multiple_of(x * GROUP + j * HD, HD)
        return remote(
            own.at[j], full.at[:, pl.ds(col, HD)], f_send.at[dx - 1, j], f_recv.at[dx - 1, j],
            (dp, y_hi * 4 + (x + dx) % 4),
        )

    locals_ = []

    def hand_out(j):
        for r in range(7):
            back(r, j).start()
        col = pl.multiple_of(me * GROUP + j * HD, HD)
        copy = pltpu.make_async_copy(send2.at[j, me], tok.at[:, pl.ds(col, HD)], self_sem.at[2 + j])
        copy.start()
        locals_.append(copy)
        col = pl.multiple_of(x * GROUP + j * HD, HD)
        copy = pltpu.make_async_copy(own.at[j], full.at[:, pl.ds(col, HD)], self_sem.at[4 + j])
        copy.start()
        locals_.append(copy)

    def hand_along(j):
        for dx in (1, 3, 2):
            along(dx, j).start()

    from_partner()
    send_merged(0, 0, other_row)
    send_merged(0, 1, other_row)
    ring_step(1, 0)
    send_merged(1, 0, other_row)
    ring_step(2, 0)
    send_merged(1, 1, other_row)
    attend(0)
    hand_out(0)
    hand_along(0)
    ring_step(1, 1)
    ring_step(3, 0)
    attend(1)
    hand_out(1)
    ring_step(2, 1)
    vel_load.wait()
    for j in range(2):
        for r in range(7):
            back(r, j).wait_recv()
    hand_along(1)
    for copy in locals_:
        copy.wait()
    keep.wait()

    near = z // 2
    side = 1 - 2 * (z % 2)
    pairs = (near, (near + 4 - side) % 4, (near + side) % 4, (near + 2) % 4)

    def quarter_copy(n, lo, way):
        pair = pairs[n]
        to = 2 * lo + pair // 2
        half = pair % 2
        col = pl.multiple_of(me * TOK, TOK)
        y_to = (y_hi + way) % 2
        return remote(
            c_send_buf.at[n, lo], quarter.at[half, :, pl.ds(col, TOK)],
            c_send.at[n, lo, way], c_recv.at[half, way * 4 + (to + 4 - x) % 4],
            (dp, y_to * 4 + to),
        )

    def local_quarter(n, lo):
        half = pairs[n] % 2
        col = pl.multiple_of(me * TOK, TOK)
        return pltpu.make_async_copy(
            c_send_buf.at[n, lo], quarter.at[half, :, pl.ds(col, TOK)], self_sem.at[6 + half]
        )

    def project(n):
        pair = pairs[n]
        for lo in range(2):
            first = pl.multiple_of(lo * 1536 + pair * 384, 384)
            weights = w_all[pl.ds(first, 384)]
            proj = dot_t(tok[...], weights)
            moved = jnp.dot(
                onehot, vel[:, pl.ds(first, 384)], preferred_element_type=jnp.float32
            )
            cot = counts * proj - moved
            c_send_buf[n, lo] = cot.T.astype(jnp.bfloat16)
            to = 2 * lo + pair // 2
            quarter_copy(n, lo, 1).start()

            @pl.when(to != x)
            def _():
                quarter_copy(n, lo, 0).start()

            @pl.when(to == x)
            def _():
                local_quarter(n, lo).start()

            part = jnp.dot(cot.astype(jnp.bfloat16), weights, preferred_element_type=jnp.float32)
            if n == 0 and lo == 0:
                acc[...] = part
            else:
                acc[...] += part

    early = (near % 2 + (near // 2 + x) % 2) % 2
    halves = (early, 1 - early)

    from_sibling(8)
    project(0)
    ring_step(4, 0)
    ring_step(3, 1, (1,))
    from_sibling(12)
    project(1)
    ring_step(3, 1, (0,))
    from_sibling(15)
    project(2)
    ring_step(4, 1)
    from_sibling(16)
    project(3)

    def grads(r):
        here = pl.ds(pl.multiple_of(me * TOK, TOK), TOK)
        return remote(
            g_buf.at[peers[r]], ga_ref.at[here], g_send.at[r], g_recv.at[r], (dp, peers[r])
        )

    for h in range(8):
        g_buf[h] = acc[:, h * GROUP : (h + 1) * GROUP].astype(jnp.bfloat16)
    for r in range(7):
        grads(r).start()
    ga_own = pltpu.make_async_copy(
        g_buf.at[me], ga_ref.at[pl.ds(pl.multiple_of(me * TOK, TOK), TOK)], self_sem.at[8]
    )
    ga_own.start()

    def half_term(half):
        for way in range(2):
            for dx in range(4):
                if way or dx:
                    col = pl.multiple_of(me * TOK, TOK)
                    remote(
                        c_send_buf.at[0, 0], quarter.at[half, :, pl.ds(col, TOK)],
                        c_send.at[0, 0, 0], c_recv.at[half, way * 4 + dx], sibling,
                    ).wait_recv()
        pltpu.make_async_copy(
            c_send_buf.at[0, 0], quarter.at[half, :, pl.ds(0, TOK)], self_sem.at[6 + half]
        ).wait()
        for block in range(4):
            part = jnp.dot(
                quarter[half], full[:, block * GROUP : (block + 1) * GROUP],
                preferred_element_type=jnp.float32,
            )
            for zi in range(2):
                for c in range(2):
                    top = zi * 192 + c * ROWS
                    term[half, c, zi, block] = part[top : top + ROWS]
                    term_out[half, c, zi, block] = part[top : top + ROWS].astype(jnp.bfloat16)
        copy = swap(half)
        copy.start()

    def swap(half):
        return remote(
            term_out.at[half, 1 - core], term_sib.at[half], b_send.at[half], b_recv.at[half], sibling
        )

    def reduce_copy(half, dz):
        turn_to = (z + dz + 7) % 8
        zi = turn_to // 4
        block = turn_to % 4
        lo = (half + block + 1) % 2
        rel = ((lo + y_lo) % 2) * 8 + dz
        return lo, zi, block, remote(
            rs_buf.at[half, zi, block], rs_recv.at[rel], r_send.at[half, dz], r_recv.at[rel],
            (dp_of(lo, (z + dz) % 8, core), me),
        )

    def spread(half):
        swap(half).wait_recv()
        for dz in (4, 3, 5, 2, 6, 1, 7, 0):
            lo, zi, block, copy = reduce_copy(half, dz)
            rs_buf[half, zi, block] = (
                term[half, core, zi, block] + term_sib[half, zi, block].astype(jnp.float32)
            ).astype(jnp.bfloat16)
            if dz:
                copy.start()
            else:

                @pl.when(lo != y_lo)
                def _():
                    copy.start()

                @pl.when(lo == y_lo)
                def _():
                    rs_recv[0] = rs_buf[half, zi, block]

    for dx in (1, 3, 2):
        for j in range(2):
            along(dx, j).wait_recv()
    half_term(halves[0])
    spread(halves[0])
    half_term(halves[1])
    spread(halves[1])

    for rel in range(1, 16):
        remote(
            rs_buf.at[0, 0, 0], rs_recv.at[rel], r_send.at[0, 0], r_recv.at[rel], sibling
        ).wait_recv()

    def add(rel, total):
        return total + rs_recv[rel].astype(jnp.float32)

    fin[...] = lax.fori_loop(0, 16, add, jnp.zeros((ROWS, GROUP), jnp.float32))
    place_copy = remote(fin, gw_ref, e_send.at[0], e_recv.at[0], dest)
    place_copy.start()

    to_partner.wait_send()
    for copy in pending:
        copy.wait_send()
    for copy in across:
        copy.wait_send()
    for r in range(7):
        for j in range(2):
            back(r, j).wait_send()
            for a in range(2):
                exchange(r, j, a).wait_send()
        grads(r).wait()
    ga_own.wait()
    for dx in (1, 3, 2):
        for j in range(2):
            along(dx, j).wait_send()
    for n in range(4):
        for lo in range(2):
            quarter_copy(n, lo, 1).wait_send()

            @pl.when(2 * lo + pairs[n] // 2 != x)
            def _():
                quarter_copy(n, lo, 0).wait_send()

    for half in range(2):
        swap(half).wait_send()
        for dz in range(8):
            lo, _, _, copy = reduce_copy(half, dz)
            if dz:
                copy.wait_send()
            else:

                @pl.when(lo != y_lo)
                def _():
                    copy.wait_send()

    place_copy.wait()


def clip_call(queries, key_states, queries_dot, keys_dot, value_states, values_dot, velocity, slot, gap, w_in):
    any_spec = pl.BlockSpec(memory_space=pl.ANY)
    vmem = pl.BlockSpec(memory_space=pltpu.VMEM)
    bf = jnp.bfloat16
    f32 = jnp.float32
    dma = pltpu.SemaphoreType.DMA
    return pl.pallas_call(
        clip_kernel,
        out_shape=(
            jax.ShapeDtypeStruct((MERGED, GROUP), bf),
            jax.ShapeDtypeStruct((ROWS, GROUP), f32),
        ),
        in_specs=[any_spec] * 7 + [vmem, pl.BlockSpec(memory_space=pltpu.SMEM), vmem],
        out_specs=(any_spec, any_spec),
        scratch_shapes=[
            pltpu.VMEM((16, F), bf),
            pltpu.VMEM((6, SRC_DEV, F), bf),
            pltpu.VMEM((SRC_DEV, D), bf),
            pltpu.VMEM((8, 2, 6, TOK, HD), bf),
            pltpu.VMEM((2, 8, 6, TOK, HD), bf),
            pltpu.VMEM((2, 8, TOK, HD), bf),
            pltpu.VMEM((2, MERGED, HD), bf),
            pltpu.VMEM((MERGED, 2 * HD), bf),
            pltpu.VMEM((MERGED, 2 * HD), bf),
            pltpu.VMEM((8, 16, F), bf),
            pltpu.VMEM((ROWS, F), bf),
            pltpu.VMEM((D, F), bf),
            pltpu.VMEM((TOK, F), bf),
            pltpu.VMEM((MERGED, 4 * GROUP), bf),
            pltpu.VMEM((TOK, F), f32),
            pltpu.VMEM((4, 2, 384, TOK), bf),
            pltpu.VMEM((2, 384, MERGED), bf),
            pltpu.VMEM((8, TOK, GROUP), bf),
            pltpu.VMEM((2, 2, 2, 4, ROWS, GROUP), f32),
            pltpu.VMEM((2, 2, 2, 4, ROWS, GROUP), bf),
            pltpu.VMEM((2, 2, 4, ROWS, GROUP), bf),
            pltpu.VMEM((2, 2, 4, ROWS, GROUP), bf),
            pltpu.VMEM((16, ROWS, GROUP), bf),
            pltpu.VMEM((ROWS, GROUP), f32),
            dma((7,)),
            dma((9,)),
            dma((7, 2, 2)),
            dma((7, 2, 2)),
            dma((7, 2)),
            dma((7, 2)),
            dma((3, 2)),
            dma((3, 2)),
            dma((7,)),
            dma((7,)),
            dma((2,)),
            dma((1,)),
            dma((1,)),
            dma((2, 4, 2)),
            dma((2, 4, 2)),
            dma((16,)),
            dma((16,)),
            dma((4, 2, 2)),
            dma((2, 8)),
            dma((7,)),
            dma((7,)),
            dma((2,)),
            dma((2,)),
            dma((2, 8)),
            dma((16,)),
            dma((1,)),
            dma((1,)),
        ],
        compiler_params=pltpu.CompilerParams(
            collective_id=0, has_side_effects=True, vmem_limit_bytes=60 << 20
        ),
        cost_estimate=pl.CostEstimate(
            flops=10_000_000_000, bytes_accessed=9 << 20, transcendentals=2 << 20
        ),
    )(
        queries, key_states, queries_dot, keys_dot, value_states, values_dot, velocity,
        slot, gap, w_in,
    )


def on_device(
    queries, key_states, value_states, queries_dot, keys_dot, values_dot,
    velocity, time_gap, merge_slot, out_weight,
):
    grad_attn, grad_weight = clip_call(
        queries[0], key_states[0], queries_dot[0], keys_dot[0], value_states[0], values_dot[0],
        velocity[0], merge_slot, time_gap.reshape(1, 1), out_weight,
    )
    return (grad_attn[None], grad_weight)


def solution(mesh):
    block = P("dp", "head", None)
    return jax.shard_map(
        on_device,
        mesh=mesh,
        in_specs=(block,) * 7 + (P("dp"), P("dp", "head"), P(("dp", "head"), None)),
        out_specs=(P("dp", None, "head"), P("dp", "head")),
        check_vma=False,
    )
```
